32 devices in a mesh: groups: 2 (over x), rows: 8 (over z, y), layers: 2 (over core).
Axes of the slice: x: 2, y: 2, z: 4, core: 2. Of those that a mesh axis runs over, the one named last changes fastest.
Arguments:
- density: bfloat16 [256, 128, 768], P(('groups', 'rows'), None, 'layers'), parts along dimension 0, may hold values from -0.8984375 to 0.8984375
- columns: int32 [256, 6], P(('groups', 'rows'), 'layers'), parts along dimension 0, may hold values from 0 to 127, as said below
- kept: int32 [256, 6], P(('groups', 'rows'), 'layers'), parts along dimension 0, may hold values from 0 to 127, as said below
Outputs:
- new_density: bfloat16 [256, 128, 768], P(('groups', 'rows'), None, 'layers'), parts along dimension 0
The draws below stay inside these ranges and needn't reach their ends.
There are 2 independent parts, one for each index of `groups`. The reference program is written for one: setup_inputs(seed, part) draws one part's arguments, and reference() takes and returns one part's arrays. A program takes and returns all parts, laid end to end along the dimension named above; each array names one. Nothing has to cross between parts.
Inputs may be any that keep to these rules, and one draw needn't show every extreme that they name: Each block row's 6 block columns are distinct and include the row itself. Block row r lies in index r // 16 of the rows axis; the block rows named by the columns of one such index's 16 block rows lie in that index or in the 2 indices on either side of it, counted around the axis; at most 2 distinct ones lie in any one other index, and exactly 2 in some. Each block row's 6 kept block columns are distinct and include the row itself.
All inputs are finite; a program needn't handle non-finite values.
Results may differ from the reference program's by a relative error of at most 0.0055.
Values may be sent and summed in bfloat16 or wider, within the bound.
No kernel may reach another device: no remote copies, remote signals or barrier semaphores. Data moves between devices by JAX's collectives and lax.ppermute only.
A program may use at most 64 MiB of HBM per device.

```python
import jax
import jax.numpy as jnp
from jax import lax

BLOCK = 128
SLOTS = 6
CAP = 2
REACH = 2
ROWS_DEV = 16
BLOCKS = 128


def shuffle_rows(key, table):
    count_rows, width = table.shape
    scores = jax.random.randint(key, (count_rows, width), 0, 1 << 16) * width + jnp.arange(width)
    order = jnp.argsort(scores, axis=-1)
    return jnp.take_along_axis(table, order, axis=-1)


def pattern(key):
    owners = BLOCKS // ROWS_DEV
    remote = SLOTS // 2
    nearby = SLOTS - 1 - remote
    keys = jax.random.split(key, 7)
    device = jnp.arange(owners)
    peer = (device[None, :] - device[:, None]) % owners
    offset = jnp.where(peer > owners // 2, peer - owners, peer)
    counts = jax.random.randint(keys[0], (owners, owners), 0, CAP + 1)
    counts = jnp.where(jnp.abs(offset) == 1, CAP, counts)
    counts = jnp.where(offset == 2, jnp.maximum(counts, 1), counts)
    counts = jnp.where((offset == 0) | (jnp.abs(offset) > REACH), 0, counts)
    pick_scores = jax.random.randint(keys[1], (owners, owners, ROWS_DEV), 0, 1 << 16) * ROWS_DEV + jnp.arange(ROWS_DEV)
    chosen = jnp.argsort(pick_scores, axis=-1)[:, :, :CAP]
    slot_ids = jnp.arange(CAP)
    valid = slot_ids[None, None, :] < counts[:, :, None]
    global_rows = device[None, :, None] * ROWS_DEV + chosen
    order_scores = jax.random.randint(keys[2], (owners, owners, CAP), 0, 1 << 16) * (owners * CAP) + device[None, :, None] * CAP + slot_ids[None, None, :] + owners * CAP
    order_scores = jnp.where(peer[:, :, None] == 1, slot_ids[None, None, :], order_scores)
    order_scores = jnp.where(valid, order_scores, 1 << 30).reshape(owners, owners * CAP)
    order = jnp.argsort(order_scores, axis=-1)
    candidates = jnp.take_along_axis(global_rows.reshape(owners, owners * CAP), order, axis=1)
    used = jnp.sum(valid.astype(jnp.int32), axis=(1, 2))
    local_ids = jnp.arange(ROWS_DEV)
    positions = (local_ids[:, None] * remote + jnp.arange(remote)[None, :])[None, :, :] % used[:, None, None]
    far_cols = jnp.take_along_axis(candidates, positions.reshape(owners, ROWS_DEV * remote), axis=1).reshape(owners, ROWS_DEV, remote)
    near_scores = jax.random.randint(keys[3], (owners, ROWS_DEV, ROWS_DEV - 1), 0, 1 << 16) * ROWS_DEV + jnp.arange(ROWS_DEV - 1)
    offsets = jnp.argsort(near_scores, axis=-1)[:, :, :nearby] + 1
    near_cols = device[:, None, None] * ROWS_DEV + (local_ids[None, :, None] + offsets) % ROWS_DEV
    self_cols = (device[:, None] * ROWS_DEV + local_ids[None, :])[:, :, None]
    row_cols = jnp.concatenate([self_cols, near_cols, far_cols], axis=-1).reshape(BLOCKS, SLOTS)
    columns = shuffle_rows(keys[4], row_cols)
    second = columns[columns].reshape(BLOCKS, SLOTS * SLOTS)
    ordered = jnp.sort(second, axis=-1)
    row_ids = jnp.arange(BLOCKS)[:, None]
    first = jnp.concatenate([jnp.ones((BLOCKS, 1), bool), ordered[:, 1:] != ordered[:, :-1]], axis=-1)
    first = first & (ordered != row_ids)
    scores = jax.random.randint(keys[5], (BLOCKS, SLOTS * SLOTS), 0, 1 << 16) * (SLOTS * SLOTS) + jnp.arange(SLOTS * SLOTS) + 1
    scores = jnp.where(first, scores, 0)
    top_values, top_ids = lax.top_k(scores, SLOTS - 1)
    picked = jnp.take_along_axis(ordered, top_ids, axis=-1)
    kept = shuffle_rows(keys[6], jnp.concatenate([row_ids, picked], axis=-1))
    return (columns.astype(jnp.int32), kept.astype(jnp.int32))


def draw_columns(key, part):
    shared = pattern(key)
    return shared[0]


def draw_kept(key, part):
    shared = pattern(key)
    return shared[1]


def block_scale(own_key, extent, shards, least, high):
    def one(dim, shards_of):
        heights = jax.random.uniform(jax.random.fold_in(jax.random.fold_in(own_key, 6), dim), (shards_of,), jnp.float32, least / len(shards), high / len(shards))
        return jnp.repeat(jnp.exp(heights), extent[dim] // shards_of).reshape((-1,) + (1,) * (len(extent) - dim - 1))

    gain = one(*shards[0])
    for cut in shards[1:]:
        gain = gain * one(*cut)
    return gain


def centred(rng, dims, scale, reach, shards=(), held_as=jnp.bfloat16):
    result = scale * jax.random.normal(rng, dims, jnp.float32)
    if shards:
        result = result * block_scale(rng, dims, shards, -0.22, 0.18)
    return jnp.clip(result, -reach, reach).astype(held_as)


def setup_inputs(seed: int = 0, part: int = 0) -> dict:
    key_of = jax.random.split(jax.random.key(seed), 4)
    own_keys = jax.random.split(jax.random.fold_in(key_of[3], part), 4)
    density = centred(own_keys[0], (BLOCKS, BLOCK, SLOTS * BLOCK), 0.15, 0.8984375, ((0, 8), (2, 2)))
    columns = draw_columns(jax.random.fold_in(jax.random.fold_in(key_of[3], part), 71), part)
    kept = draw_kept(jax.random.fold_in(jax.random.fold_in(key_of[3], part), 71), part)
    return dict(density=density, columns=columns, kept=kept)


def filtered(left, left_cols, right, right_cols, targets):
    def one_row(row_id):
        left_blocks = left[row_id].reshape(BLOCK, SLOTS, BLOCK).astype(jnp.float32)
        picks = left_cols[row_id]
        right_rows = right[picks].astype(jnp.float32)
        partial_value = jnp.einsum('xay,ayz->axz', left_blocks, right_rows, precision=lax.Precision.HIGHEST)
        partial_value = partial_value.reshape(SLOTS, BLOCK, SLOTS, BLOCK)
        picked_cols = right_cols[picks]
        matched = (picked_cols[:, :, None] == targets[row_id][None, None, :]).astype(jnp.float32)
        summed = jnp.einsum('axbz,abs->xsz', partial_value, matched, precision=lax.Precision.HIGHEST)
        return summed.reshape(BLOCK, SLOTS * BLOCK)

    return lax.map(one_row, jnp.arange(BLOCKS, dtype=jnp.int32))


def reference(density, columns, kept):
    square = filtered(density, columns, density, columns, kept).astype(jnp.bfloat16)
    cube = filtered(density, columns, square, kept, kept)
    return (3.0 * square.astype(jnp.float32) - 2.0 * cube).astype(jnp.bfloat16)
```

```python
import functools

import jax
import jax.numpy as jnp
from jax import lax
from jax.experimental import pallas as pl
from jax.experimental.pallas import tpu as pltpu
from jax.sharding import PartitionSpec as P

CAP = 2
REACH = 2
OFFSETS = tuple(step for reach in range(1, REACH + 1) for step in (reach, -reach))
VMEM_LIMIT = 24 * 1024 * 1024


def from_ahead(value, steps):
    count = lax.axis_size("rows")
    pairs = [(source, (source - steps) % count) for source in range(count)]
    return lax.ppermute(value, "rows", pairs)


def from_sibling(value):
    return lax.ppermute(value, "layers", [(0, 1), (1, 0)])


def named_rows(columns, owner, block_rows):
    local = columns.reshape(-1) - owner * block_rows
    inside = (local >= 0) & (local < block_rows)
    low = jnp.min(jnp.where(inside, local, block_rows - 1))
    high = jnp.max(jnp.where(inside, local, 0))
    return jnp.stack([low, high]).astype(jnp.int32)


def pick_rows(table, rows):
    hit = rows[:, None, None] == jnp.arange(table.shape[0], dtype=jnp.int32)[None, :, None]
    return jnp.sum(jnp.where(hit, table[None], 0), axis=1)


def block_index(columns, targets, right_cols, slots, half, segments):
    rows, width = columns.shape
    entries = jnp.arange(right_cols.shape[0], dtype=jnp.int32)
    hit = slots[:, :, None] == entries[None, None, :]
    met = jnp.sum(jnp.where(hit[..., None], right_cols[None, None], 0), axis=2)
    own = rows
    far = right_cols.shape[0] - rows
    base = jnp.where(slots < own, slots, slots + own)
    shift = jnp.where(slots < own, own, far)
    empty = segments - 1
    terms = []
    for b in range(width):
        where_b = (b % half) * segments + base + (shift if b >= half else 0)
        terms.append(
            jnp.where(
                met[:, :, b, None] == targets[:, None, :],
                where_b[:, :, None] - empty,
                0,
            )
        )
    return (sum(terms) + empty).reshape(-1).astype(jnp.int32)


def fill(table, parts, sems, half, edge, segments, first):
    copies = []
    begin = 0
    for part in parts:
        size = part.shape[0]
        for b in range(half):
            copies.append(
                pltpu.make_async_copy(
                    part.at[:, :, pl.ds(b * edge, edge)],
                    table.at[pl.ds(b * segments + begin, size)],
                    sems.at[first + len(copies)],
                )
            )
        begin += size
    for copy in copies:
        copy.start()
    return copies


def gather_kernel(rows_ref, density_ref, *refs):
    outs, sems = refs[:-1], refs[-1]
    copies = []
    for position, out in enumerate(outs):
        for k in range(CAP):
            n = position * CAP + k
            copies.append(
                pltpu.make_async_copy(density_ref.at[rows_ref[n]], out.at[k], sems.at[n])
            )
    for copy in copies:
        copy.start()
    for copy in copies:
        copy.wait()


def gather(rows, density):
    piece = jax.ShapeDtypeStruct((CAP,) + density.shape[1:], density.dtype)
    return pl.pallas_call(
        gather_kernel,
        out_shape=[piece] * len(OFFSETS),
        in_specs=[pl.BlockSpec(memory_space=pltpu.SMEM), pl.BlockSpec(memory_space=pl.ANY)],
        out_specs=[pl.BlockSpec(memory_space=pl.ANY)] * len(OFFSETS),
        scratch_shapes=[pltpu.SemaphoreType.DMA((len(OFFSETS) * CAP,))],
        name="gather_rows",
    )(rows, density)


def row_product(table, index_ref, base, left, width, half, edge):
    total = None
    for a in range(0, width, 2):
        pair = range(a, min(a + 2, width))
        lhs = jnp.concatenate([left(k) for k in pair], axis=1)
        rhs = jnp.concatenate(
            [
                jnp.concatenate(
                    [table[index_ref[base + k * half + s]] for s in range(half)], axis=1
                )
                for k in pair
            ],
            axis=0,
        )
        term = jnp.dot(lhs, rhs, preferred_element_type=jnp.float32)
        total = term if total is None else total + term
    return total


def square_kernel(own, edge, half, segments, wanted, rows_ref, index_ref, *refs):
    parts = refs[: 2 + 2 * len(OFFSETS)]
    outs = refs[len(parts) : -2]
    table, sems = refs[-2:]
    copies = fill(table, parts, sems, half, edge, segments, 0)
    width = 2 * half
    for b in range(half):
        table[b * segments + segments - 1] = jnp.zeros((edge, edge), table.dtype)
    for copy in copies:
        copy.wait()

    def one(i, out, place):
        row = rows_ref[i] if wanted else i
        left = lambda k: table[(k % half) * segments + (k // half) * own + row]
        total = row_product(table, index_ref, row * (width * half), left, width, half, edge)
        out[place] = total.astype(out.dtype)

    if wanted:
        for position, out in enumerate(outs):
            for k in range(CAP):
                one(position * CAP + k, out, k)
    else:

        def body(i, carry):
            one(i, outs[0], i)
            return carry

        lax.fori_loop(0, own, body, 0, unroll=2)


def square(rows, index, parts, wanted):
    own, edge, wide = parts[0].shape
    half = wide // edge
    segments = 2 * own + 2 * len(OFFSETS) * CAP + 1
    if wanted:
        shapes = [jax.ShapeDtypeStruct((CAP, edge, wide), parts[0].dtype)] * len(OFFSETS)
        count = len(OFFSETS) * CAP
    else:
        shapes = [jax.ShapeDtypeStruct((own, edge, wide), parts[0].dtype)]
        count = own
    return pl.pallas_call(
        functools.partial(square_kernel, own, edge, half, segments, wanted),
        out_shape=shapes,
        in_specs=[pl.BlockSpec(memory_space=pltpu.SMEM)] * 2
        + [pl.BlockSpec(memory_space=pl.ANY)] * len(parts),
        out_specs=[pl.BlockSpec(memory_space=pltpu.VMEM)] * len(shapes),
        scratch_shapes=[
            pltpu.VMEM((half * segments, edge, edge), parts[0].dtype),
            pltpu.SemaphoreType.DMA((half * len(parts),)),
        ],
        compiler_params=pltpu.CompilerParams(vmem_limit_bytes=VMEM_LIMIT),
        cost_estimate=pl.CostEstimate(
            flops=count * 2 * edge * 2 * wide * wide,
            bytes_accessed=5 * 1024 * 1024,
            transcendentals=0,
        ),
        name="square_wanted" if wanted else "square_rows",
    )(rows, index, *parts)


def cube_kernel(own, edge, half, segments, index_ref, left_own, left_other, *refs):
    out, table, lefts, sems = refs[-4:]
    parts = refs[:-4]
    copies = fill(table, parts, sems, half, edge, segments, 0)
    copies += fill(lefts, (left_own, left_other), sems, half, edge, 2 * own, len(copies))
    width = 2 * half
    for b in range(half):
        table[b * segments + segments - 1] = jnp.zeros((edge, edge), table.dtype)
    for copy in copies:
        copy.wait()

    def body(i, carry):
        left = lambda k: lefts[(k % half) * (2 * own) + (k // half) * own + i]
        total = row_product(table, index_ref, i * (width * half), left, width, half, edge)
        first = jnp.concatenate([table[s * segments + i] for s in range(half)], axis=1)
        out[i] = (3.0 * first.astype(jnp.float32) - 2.0 * total).astype(out.dtype)
        return carry

    lax.fori_loop(0, own, body, 0, unroll=2)


def cube(index, left_own, left_other, parts):
    own, edge, wide = left_own.shape
    half = wide // edge
    segments = 2 * own + 2 * len(OFFSETS) * CAP + 1
    return pl.pallas_call(
        functools.partial(cube_kernel, own, edge, half, segments),
        out_shape=jax.ShapeDtypeStruct(left_own.shape, left_own.dtype),
        in_specs=[pl.BlockSpec(memory_space=pltpu.SMEM)]
        + [pl.BlockSpec(memory_space=pl.ANY)] * (len(parts) + 2),
        out_specs=pl.BlockSpec(memory_space=pltpu.VMEM),
        scratch_shapes=[
            pltpu.VMEM((half * segments, edge, edge), left_own.dtype),
            pltpu.VMEM((half * 2 * own, edge, edge), left_own.dtype),
            pltpu.SemaphoreType.DMA((half * (len(parts) + 2),)),
        ],
        compiler_params=pltpu.CompilerParams(vmem_limit_bytes=VMEM_LIMIT),
        cost_estimate=pl.CostEstimate(
            flops=own * 2 * edge * 2 * wide * wide,
            bytes_accessed=9 * 1024 * 1024,
            transcendentals=0,
        ),
        name="cube_rows",
    )(index, left_own, left_other, *parts)


def local(density, columns, kept):
    own, edge, wide = density.shape
    half = columns.shape[1]
    peers = lax.axis_size("rows")
    me = lax.axis_index("rows")

    numbers = jnp.concatenate([columns, kept], axis=1)
    other_numbers = from_sibling(numbers)
    all_columns = jnp.concatenate([columns, other_numbers[:, :half]], axis=1)
    all_kept = jnp.concatenate([kept, other_numbers[:, half:]], axis=1)
    all_numbers = jnp.concatenate([all_columns, all_kept], axis=1)
    near = {step: from_ahead(all_numbers, step) for step in OFFSETS}
    other_density = from_sibling(density)

    width = 2 * half
    sends = jnp.concatenate([named_rows(near[-step][:, :width], me, own) for step in OFFSETS])
    wants = [named_rows(all_columns, (me + step) % peers, own) for step in OFFSETS]

    got = [
        from_ahead(piece, step)
        for step, piece in zip(OFFSETS, gather(sends, density))
    ]
    got_other = [from_sibling(piece) for piece in got]

    owner = all_columns // own
    distance = (owner - me) % peers
    slots = all_columns - me * own
    for position, (step, want) in enumerate(zip(OFFSETS, wants)):
        local_row = all_columns - ((me + step) % peers) * own
        slots = jnp.where(
            distance == step % peers,
            own + position * CAP + (local_row != want[0]).astype(jnp.int32),
            slots,
        )
    far = jnp.concatenate(
        [pick_rows(near[step], want) for step, want in zip(OFFSETS, wants)], axis=0
    )
    segments = 2 * own + 2 * len(OFFSETS) * CAP + 1
    square_index = block_index(
        all_columns, kept, jnp.concatenate([all_columns, far[:, :width]]), slots, half, segments
    )
    cube_index = block_index(
        all_columns, kept, jnp.concatenate([all_kept, far[:, width:]]), slots, half, segments
    )

    parts = [density, other_density, *got, *got_other]
    wanted = square(sends, square_index, parts, True)
    got_square = [from_ahead(piece, step) for step, piece in zip(OFFSETS, wanted)]
    (squares,) = square(sends, square_index, parts, False)
    other_squares = from_sibling(squares)
    got_square_other = [from_sibling(piece) for piece in got_square]
    return cube(
        cube_index,
        density,
        other_density,
        [squares, other_squares, *got_square, *got_square_other],
    )


def solution(mesh):
    in_specs = (
        P(("groups", "rows"), None, "layers"),
        P(("groups", "rows"), "layers"),
        P(("groups", "rows"), "layers"),
    )
    out_specs = P(("groups", "rows"), None, "layers")
    return jax.shard_map(local, mesh=mesh, in_specs=in_specs, out_specs=out_specs, check_vma=False)
```

```python
import functools

import jax
import jax.numpy as jnp
from jax import lax
from jax.experimental import pallas as pl
from jax.experimental.pallas import tpu as pltpu
from jax.sharding import PartitionSpec as P

CAP = 2
REACH = 2
OFFSETS = tuple(step for reach in range(1, REACH + 1) for step in (reach, -reach))
BEHIND = tuple(OFFSETS.index(-step) for step in OFFSETS)
SUBLANES, LANES = 8, 128
VMEM_LIMIT = 24 * 1024 * 1024


def from_ahead(value, steps):
    count = lax.axis_size("rows")
    pairs = [(source, (source - steps) % count) for source in range(count)]
    return lax.ppermute(value, "rows", pairs)


def from_sibling(value):
    return lax.ppermute(value, "layers", [(0, 1), (1, 0)])


def spread(columns, kept):
    table = jnp.concatenate([columns, kept], axis=1).T
    return jnp.pad(table, ((0, SUBLANES - table.shape[0]), (0, LANES - table.shape[1])))


def named_rows(own_slots, other_slots, owner, own):
    low, high = [], []
    for slots in (own_slots, other_slots):
        local = slots - owner * own
        lane = lax.broadcasted_iota(jnp.int32, local.shape, 1)
        inside = (local >= 0) & (local < own) & (lane < own)
        low.append(jnp.where(inside, local, own - 1))
        high.append(jnp.where(inside, local, 0))
    return jnp.minimum(*low), jnp.maximum(*high)


def fill(table, parts, sems, half, edge, segments, first):
    copies = []
    begin = 0
    for part in parts:
        size = part.shape[0]
        for b in range(half):
            copies.append(
                pltpu.make_async_copy(
                    part.at[:, :, pl.ds(b * edge, edge)],
                    table.at[pl.ds(b * segments + begin, size)],
                    sems.at[first + len(copies)],
                )
            )
        begin += size
    for copy in copies:
        copy.start()
    return copies


def gather_kernel(own, half, density_ref, *refs):
    near, (rows_ref, *outs), sems = refs[: len(OFFSETS)], refs[len(OFFSETS) : -1], refs[-1]
    me = lax.axis_index("rows")
    copies = []
    for position, out in enumerate(outs):
        numbers = near[BEHIND[position]]
        low, high = named_rows(
            numbers[0:half], numbers[SUBLANES : SUBLANES + half], me, own
        )
        for k, row in enumerate((jnp.min(low), jnp.max(high))):
            n = position * CAP + k
            rows_ref[n] = row
            copies.append(pltpu.make_async_copy(density_ref.at[row], out.at[k], sems.at[n]))
            copies[-1].start()
    for copy in copies:
        copy.wait()


def gather(density, near, half):
    piece = jax.ShapeDtypeStruct((CAP,) + density.shape[1:], density.dtype)
    return pl.pallas_call(
        functools.partial(gather_kernel, density.shape[0], half),
        out_shape=[jax.ShapeDtypeStruct((len(OFFSETS) * CAP,), jnp.int32)]
        + [piece] * len(OFFSETS),
        in_specs=[pl.BlockSpec(memory_space=pl.ANY)]
        + [pl.BlockSpec(memory_space=pltpu.VMEM)] * len(OFFSETS),
        out_specs=[pl.BlockSpec(memory_space=pltpu.SMEM)]
        + [pl.BlockSpec(memory_space=pltpu.VMEM)] * len(OFFSETS),
        scratch_shapes=[pltpu.SemaphoreType.DMA((len(OFFSETS) * CAP,))],
        compiler_params=pltpu.CompilerParams(vmem_limit_bytes=VMEM_LIMIT),
        cost_estimate=pl.CostEstimate(flops=0, bytes_accessed=1024 * 1024, transcendentals=0),
        name="gather_rows",
    )(density, *near)


def tables_kernel(own, half, peers, segments, mine_ref, *refs):
    near, (square_ref, cube_ref) = refs[: len(OFFSETS)], refs[len(OFFSETS) :]
    me = lax.axis_index("rows")
    shape = (SUBLANES, LANES)
    lane = lax.broadcasted_iota(jnp.int32, shape, 1)
    own_columns, own_kept = mine_ref[0:half], mine_ref[half : 2 * half]
    other_columns = mine_ref[SUBLANES : SUBLANES + half]
    other_kept = mine_ref[SUBLANES + half : SUBLANES + 2 * half]
    pad = jnp.zeros((SUBLANES - 2 * half, LANES), jnp.int32)
    columns = jnp.concatenate([own_columns, other_columns, pad], axis=0)
    column_table = columns
    kept_table = jnp.concatenate([own_kept, other_kept, pad], axis=0)
    slots = columns - me * own
    for position, step in enumerate(OFFSETS):
        owner = lax.rem(me + step + peers, peers)
        low, high = named_rows(own_columns, other_columns, owner, own)
        low = jnp.min(jnp.min(low, axis=0, keepdims=True), axis=1, keepdims=True)
        high = jnp.max(jnp.max(high, axis=0, keepdims=True), axis=1, keepdims=True)
        local = columns - owner * own
        first = own + position * CAP
        slots = jnp.where(
            (local >= 0) & (local < own), first + (local != low).astype(jnp.int32), slots
        )
        numbers = near[position]
        far_columns = jnp.concatenate([numbers[0:half], numbers[SUBLANES : SUBLANES + half], pad])
        far_kept = jnp.concatenate(
            [numbers[half : 2 * half], numbers[SUBLANES + half : SUBLANES + 2 * half], pad]
        )
        source = jnp.where(lane == first, low, high)
        here = (lane == first) | (lane == first + 1)
        column_table = jnp.where(
            here, jnp.take_along_axis(far_columns, source, axis=1), column_table
        )
        kept_table = jnp.where(here, jnp.take_along_axis(far_kept, source, axis=1), kept_table)
    slots = jnp.where(lane < own, jnp.clip(slots, 0, LANES - 1), 0)
    far = len(OFFSETS) * CAP
    base = jnp.where(slots < own, slots, slots + own)
    shift = jnp.where(slots < own, own, far)
    empty = half * segments - 1
    for out, table in ((square_ref, column_table), (cube_ref, kept_table)):
        met = [
            jnp.take_along_axis(jnp.broadcast_to(table[b : b + 1], shape), slots, axis=1)
            for b in range(2 * half)
        ]
        for s in range(half):
            index = jnp.full(shape, empty, jnp.int32)
            for b in range(2 * half):
                place = (b % half) * segments + base + (shift if b >= half else 0)
                index = jnp.where(met[b] == own_kept[s : s + 1], place, index)
            out[s * SUBLANES : (s + 1) * SUBLANES] = index


def tables(mine, near, own, half, peers, segments):
    shape = jax.ShapeDtypeStruct((half * SUBLANES, LANES), jnp.int32)
    return pl.pallas_call(
        functools.partial(tables_kernel, own, half, peers, segments),
        out_shape=[shape] * 2,
        cost_estimate=pl.CostEstimate(flops=0, bytes_accessed=64 * 1024, transcendentals=0),
        name="block_tables",
    )(mine, *near)


def row_product(table, index_ref, row, left, width, half, edge):
    total = None
    for a in range(0, width, 2):
        pair = range(a, min(a + 2, width))
        lhs = jnp.concatenate([left(k) for k in pair], axis=1)
        rhs = jnp.concatenate(
            [
                jnp.concatenate(
                    [table[index_ref[s * SUBLANES + k, row]] for s in range(half)], axis=1
                )
                for k in pair
            ],
            axis=0,
        )
        term = jnp.dot(lhs, rhs, preferred_element_type=jnp.float32)
        total = term if total is None else total + term
    return total


def square_kernel(own, edge, half, segments, wanted, rows_ref, index_ref, *refs):
    parts = refs[: 2 + 2 * len(OFFSETS)]
    outs = refs[-2 - (len(OFFSETS) if wanted else 1) : -2]
    table, sems = refs[-2:]
    copies = fill(table, parts, sems, half, edge, segments, 0)
    width = 2 * half
    table[half * segments - 1] = jnp.zeros((edge, edge), table.dtype)
    for copy in copies:
        copy.wait()

    def one(i, out, place):
        row = rows_ref[i] if wanted else i
        left = lambda k: table[(k % half) * segments + (k // half) * own + row]
        total = row_product(table, index_ref, row, left, width, half, edge)
        out[place] = total.astype(out.dtype)

    if wanted:
        for position, out in enumerate(outs):
            for k in range(CAP):
                one(position * CAP + k, out, k)
    else:

        def body(i, carry):
            one(i, outs[0], i)
            return carry

        lax.fori_loop(0, own, body, 0, unroll=2)


def square(rows, index, parts, wanted, after=()):
    own, edge, wide = parts[0].shape
    half = wide // edge
    segments = 2 * own + 2 * len(OFFSETS) * CAP + 1
    if wanted:
        shapes = [jax.ShapeDtypeStruct((CAP, edge, wide), parts[0].dtype)] * len(OFFSETS)
        count = len(OFFSETS) * CAP
    else:
        shapes = [jax.ShapeDtypeStruct((own, edge, wide), parts[0].dtype)]
        count = own
    return pl.pallas_call(
        functools.partial(square_kernel, own, edge, half, segments, wanted),
        out_shape=shapes,
        in_specs=[pl.BlockSpec(memory_space=pltpu.SMEM)] * 2
        + [pl.BlockSpec(memory_space=pl.ANY)] * (len(parts) + len(after)),
        out_specs=[pl.BlockSpec(memory_space=pltpu.VMEM)] * len(shapes),
        scratch_shapes=[
            pltpu.VMEM((half * segments, edge, edge), parts[0].dtype),
            pltpu.SemaphoreType.DMA((half * len(parts),)),
        ],
        compiler_params=pltpu.CompilerParams(vmem_limit_bytes=VMEM_LIMIT),
        cost_estimate=pl.CostEstimate(
            flops=count * 2 * edge * 2 * wide * wide,
            bytes_accessed=5 * 1024 * 1024,
            transcendentals=0,
        ),
        name="square_wanted" if wanted else "square_rows",
    )(rows, index, *parts, *after)


def cube_kernel(own, edge, half, segments, index_ref, left_own, left_other, *refs):
    out, table, lefts, sems = refs[-4:]
    parts = refs[:-4]
    copies = fill(table, parts, sems, half, edge, segments, 0)
    copies += fill(lefts, (left_own, left_other), sems, half, edge, 2 * own, len(copies))
    width = 2 * half
    table[half * segments - 1] = jnp.zeros((edge, edge), table.dtype)
    for copy in copies:
        copy.wait()

    def body(i, carry):
        left = lambda k: lefts[(k % half) * (2 * own) + (k // half) * own + i]
        total = row_product(table, index_ref, i, left, width, half, edge)
        first = jnp.concatenate([table[s * segments + i] for s in range(half)], axis=1)
        out[i] = (3.0 * first.astype(jnp.float32) - 2.0 * total).astype(out.dtype)
        return carry

    lax.fori_loop(0, own, body, 0, unroll=2)


def cube(index, left_own, left_other, parts):
    own, edge, wide = left_own.shape
    half = wide // edge
    segments = 2 * own + 2 * len(OFFSETS) * CAP + 1
    return pl.pallas_call(
        functools.partial(cube_kernel, own, edge, half, segments),
        out_shape=jax.ShapeDtypeStruct(left_own.shape, left_own.dtype),
        in_specs=[pl.BlockSpec(memory_space=pltpu.SMEM)]
        + [pl.BlockSpec(memory_space=pl.ANY)] * (len(parts) + 2),
        out_specs=pl.BlockSpec(memory_space=pltpu.VMEM),
        scratch_shapes=[
            pltpu.VMEM((half * segments, edge, edge), left_own.dtype),
            pltpu.VMEM((half * 2 * own, edge, edge), left_own.dtype),
            pltpu.SemaphoreType.DMA((half * (len(parts) + 2),)),
        ],
        compiler_params=pltpu.CompilerParams(vmem_limit_bytes=VMEM_LIMIT),
        cost_estimate=pl.CostEstimate(
            flops=own * 2 * edge * 2 * wide * wide,
            bytes_accessed=9 * 1024 * 1024,
            transcendentals=0,
        ),
        name="cube_rows",
    )(index, left_own, left_other, *parts)


def local(density, columns, kept):
    own, edge, wide = density.shape
    half = columns.shape[1]
    peers = lax.axis_size("rows")
    numbers = spread(columns, kept)
    mine = jnp.concatenate([numbers, from_sibling(numbers)], axis=0)
    near = [from_ahead(mine, step) for step in OFFSETS]
    other_density = from_sibling(density)
    sends, *pieces = gather(density, near, half)
    got = [from_ahead(piece, step) for step, piece in zip(OFFSETS, pieces)]
    got_other = [from_sibling(piece) for piece in got]
    segments = 2 * own + 2 * len(OFFSETS) * CAP + 1
    square_index, cube_index = tables(mine, near, own, half, peers, segments)

    parts = [density, other_density, *got, *got_other]
    wanted = square(sends, square_index, parts, True)
    got_square = [from_ahead(piece, step) for step, piece in zip(OFFSETS, wanted)]
    (squares,) = square(sends, square_index, parts, False, wanted[:1])
    other_squares = from_sibling(squares)
    got_square_other = [from_sibling(piece) for piece in got_square]
    return cube(
        cube_index,
        density,
        other_density,
        [squares, other_squares, *got_square, *got_square_other],
    )


def solution(mesh):
    in_specs = (
        P(("groups", "rows"), None, "layers"),
        P(("groups", "rows"), "layers"),
        P(("groups", "rows"), "layers"),
    )
    out_specs = P(("groups", "rows"), None, "layers")
    return jax.shard_map(local, mesh=mesh, in_specs=in_specs, out_specs=out_specs, check_vma=False)
```

```python
import functools

import jax
import jax.numpy as jnp
from jax import lax
from jax.experimental import pallas as pl
from jax.experimental.pallas import tpu as pltpu
from jax.sharding import PartitionSpec as P

CAP = 2
REACH = 2
OFFSETS = tuple(step for reach in range(1, REACH + 1) for step in (reach, -reach))
FAR = len(OFFSETS) * CAP
SUBLANES, LANES = 8, 128
VMEM_LIMIT = 40 * 1024 * 1024
PARAMS = pltpu.CompilerParams(vmem_limit_bytes=VMEM_LIMIT)
VMEM = pl.BlockSpec(memory_space=pltpu.VMEM)
SMEM = pl.BlockSpec(memory_space=pltpu.SMEM)


def cost(flops, size):
    return pl.CostEstimate(flops=flops, bytes_accessed=size, transcendentals=0)


def like(value):
    return jax.ShapeDtypeStruct(value.shape, value.dtype)


def from_ahead(value, steps):
    count = lax.axis_size("rows")
    pairs = [(source, (source - steps) % count) for source in range(count)]
    return lax.ppermute(value, "rows", pairs)


def from_sibling(value):
    return lax.ppermute(value, "layers", [(0, 1), (1, 0)])


def everyones(columns, kept):
    table = jnp.concatenate([columns, kept], axis=1).T
    table = jnp.pad(table, ((0, SUBLANES - table.shape[0]), (0, LANES - table.shape[1])))
    count = lax.axis_size("rows") * lax.axis_size("layers")
    table = jnp.broadcast_to(table[None], (count,) + table.shape)
    return lax.all_to_all(table, ("rows", "layers"), 0, 0, tiled=True)


def named_rows(slots_of_both, owner, own):
    low, high = [], []
    for slots in slots_of_both:
        local = slots - owner * own
        lane = lax.broadcasted_iota(jnp.int32, local.shape, 1)
        inside = (local >= 0) & (local < own) & (lane < own)
        low.append(jnp.where(inside, local, own - 1))
        high.append(jnp.where(inside, local, 0))
    return jnp.minimum(*low), jnp.maximum(*high)


def gather_kernel(own, half, peers, density_ref, numbers_ref, rows_ref, *refs):
    outs, sems = refs[:-1], refs[-1]
    me = lax.axis_index("rows")
    copies = []
    for position, out in enumerate(outs):
        reader = lax.rem(me - OFFSETS[position] + peers, peers)
        both = [numbers_ref[2 * reader + layer][0:half] for layer in range(2)]
        low, high = named_rows(both, me, own)
        for k, row in enumerate((jnp.min(low), jnp.max(high))):
            n = position * CAP + k
            rows_ref[n] = row
            copies.append(pltpu.make_async_copy(density_ref.at[row], out.at[k], sems.at[n]))
            copies[-1].start()
    for copy in copies:
        copy.wait()


def gather(density, numbers, half):
    own, edge, wide = density.shape
    piece = jax.ShapeDtypeStruct((CAP, edge, wide), density.dtype)
    return pl.pallas_call(
        functools.partial(gather_kernel, own, half, lax.axis_size("rows")),
        out_shape=[jax.ShapeDtypeStruct((FAR,), jnp.int32)] + [piece] * len(OFFSETS),
        in_specs=[pl.BlockSpec(memory_space=pltpu.HBM), VMEM],
        out_specs=[SMEM] + [VMEM] * len(OFFSETS),
        scratch_shapes=[pltpu.SemaphoreType.DMA((FAR,))],
        compiler_params=PARAMS,
        cost_estimate=cost(0, 2 * FAR * edge * wide * 2),
        name="gather_rows",
    )(density, numbers)


def stack(table, own_ref, other_ref, sems):
    own = own_ref.shape[0]
    copies = [
        pltpu.make_async_copy(own_ref, table.at[pl.ds(0, own)], sems.at[0]),
        pltpu.make_async_copy(other_ref, table.at[pl.ds(own, own)], sems.at[1]),
    ]
    for copy in copies:
        copy.start()
    table[table.shape[0] - 1] = jnp.zeros(table.shape[1:], table.dtype)
    return copies


def tables_kernel(half, peers, numbers_ref, own_ref, other_ref, *refs):
    square_ref, cube_ref, table_ref, sems = refs
    own, edge, wide = own_ref.shape
    copies = stack(table_ref, own_ref, other_ref, sems)
    me, layer = lax.axis_index("rows"), lax.axis_index("layers")
    shape = (SUBLANES, LANES)
    lane = lax.broadcasted_iota(jnp.int32, shape, 1)
    pad = jnp.zeros((SUBLANES - 2 * half, LANES), jnp.int32)

    def slots_of(device):
        first, second = numbers_ref[2 * device + layer], numbers_ref[2 * device + 1 - layer]
        return [
            jnp.concatenate([first[k : k + half], second[k : k + half], pad], axis=0)
            for k in (0, half)
        ]

    columns, kept = slots_of(me)
    named = (columns[0:half], columns[half : 2 * half])
    column_table, kept_table = columns, kept
    slots = columns - me * own
    for position, step in enumerate(OFFSETS):
        owner = lax.rem(me + step + peers, peers)
        low, high = named_rows(named, owner, own)
        low = jnp.min(jnp.min(low, axis=0, keepdims=True), axis=1, keepdims=True)
        high = jnp.max(jnp.max(high, axis=0, keepdims=True), axis=1, keepdims=True)
        local = columns - owner * own
        first = own + position * CAP
        slots = jnp.where(
            (local >= 0) & (local < own), first + (local != low).astype(jnp.int32), slots
        )
        far_columns, far_kept = slots_of(owner)
        source = jnp.where(lane == first, low, high)
        here = (lane == first) | (lane == first + 1)
        column_table = jnp.where(
            here, jnp.take_along_axis(far_columns, source, axis=1), column_table
        )
        kept_table = jnp.where(here, jnp.take_along_axis(far_kept, source, axis=1), kept_table)
    slots = jnp.where(lane < own, jnp.clip(slots, 0, LANES - 1), 0)
    stride = table_stride(half, edge)
    base = jnp.where(slots < own, slots, slots + own)
    shift = jnp.where(slots < own, own, FAR)
    empty = (table_ref.shape[0] - 1) * stride
    for out, table in ((square_ref, column_table), (cube_ref, kept_table)):
        met = [
            jnp.take_along_axis(jnp.broadcast_to(table[b : b + 1], shape), slots, axis=1)
            for b in range(2 * half)
        ]
        for s in range(half):
            index = jnp.full(shape, empty, jnp.int32)
            for b in range(2 * half):
                entry = base + shift if b >= half else base
                place = entry * stride + (b % half) * edge
                index = jnp.where(met[b] == kept[s : s + 1], place, index)
            out[s * SUBLANES : (s + 1) * SUBLANES] = index
    for copy in copies:
        copy.wait()


def table_stride(half, edge):
    return edge << (half - 1).bit_length()


def table_like(own):
    return jax.ShapeDtypeStruct((2 * own.shape[0] + 2 * FAR + 1,) + own.shape[1:], own.dtype)


def tables(numbers, own, other, half):
    shape = jax.ShapeDtypeStruct((half * SUBLANES, LANES), jnp.int32)
    return pl.pallas_call(
        functools.partial(tables_kernel, half, lax.axis_size("rows")),
        out_shape=[shape, shape, table_like(own)],
        in_specs=[VMEM] * 3,
        out_specs=[VMEM] * 3,
        scratch_shapes=[pltpu.SemaphoreType.DMA((2,))],
        compiler_params=PARAMS,
        cost_estimate=cost(0, 4 * own.size * 2),
        name="block_tables",
    )(numbers, own, other)


def stack_kernel(own_ref, other_ref, table_ref, sems):
    for copy in stack(table_ref, own_ref, other_ref, sems):
        copy.wait()


def stacked(own, other):
    return pl.pallas_call(
        stack_kernel,
        out_shape=table_like(own),
        in_specs=[VMEM] * 2,
        out_specs=VMEM,
        scratch_shapes=[pltpu.SemaphoreType.DMA((2,))],
        compiler_params=PARAMS,
        cost_estimate=cost(0, 4 * own.size * 2),
        name="stack_squares",
    )(own, other)


def add_far(table, pieces, own):
    for position, piece in enumerate(pieces):
        for k in range(CAP):
            table[2 * own + position * CAP + k] = piece[k]


def row_product(table, index_ref, row, own_ref, other_ref, half, edge):
    stride = table_stride(half, edge)

    def left(k):
        ref = own_ref if k < half else other_ref
        return ref[row, :, (k % half) * edge : (k % half + 1) * edge]

    def right(k, s):
        place = index_ref[s * SUBLANES + k, row]
        begin = pl.multiple_of(lax.bitwise_and(place, stride - 1), edge)
        return table[lax.div(place, stride), :, pl.ds(begin, edge)]

    total = None
    for a in range(0, 2 * half, 2):
        pair = range(a, min(a + 2, 2 * half))
        lhs = jnp.concatenate([left(k) for k in pair], axis=1)
        rhs = jnp.concatenate(
            [jnp.concatenate([right(k, s) for s in range(half)], axis=1) for k in pair], axis=0
        )
        term = jnp.dot(lhs, rhs, preferred_element_type=jnp.float32)
        total = term if total is None else total + term
    return total


def square_kernel(half, index_ref, rows_ref, own_ref, other_ref, *refs):
    pieces = refs[1 : 1 + 2 * len(OFFSETS)]
    out, *wanted, table = refs[1 + len(pieces) :]
    own, edge, wide = own_ref.shape
    add_far(table, pieces, own)

    def body(i, carry):
        total = row_product(table, index_ref, i, own_ref, other_ref, half, edge)
        out[i] = total.astype(out.dtype)
        return carry

    lax.fori_loop(0, own, body, 0, unroll=2)
    for position, piece in enumerate(wanted):
        for k in range(CAP):
            piece[k] = out[rows_ref[position * CAP + k]]


def square(index, rows, own, other, table, pieces, half):
    size, edge, wide = own.shape
    piece = jax.ShapeDtypeStruct((CAP, edge, wide), own.dtype)
    count = len(OFFSETS)
    out = pl.pallas_call(
        functools.partial(square_kernel, half),
        out_shape=[like(own), *([piece] * count), like(table)],
        in_specs=[SMEM] * 2 + [VMEM] * (3 + len(pieces)),
        out_specs=[VMEM] * (2 + count),
        input_output_aliases={4: 1 + count},
        compiler_params=PARAMS,
        cost_estimate=cost(size * 4 * edge * wide * wide, 8 * own.size * 2),
        name="square_rows",
    )(index, rows, own, other, table, *pieces)
    return out[0], out[1 : 1 + count]


def cube_kernel(half, index_ref, own_ref, other_ref, *refs):
    pieces = refs[1 : 1 + 2 * len(OFFSETS)]
    out, table = refs[1 + len(pieces) :]
    own, edge, wide = own_ref.shape
    add_far(table, pieces, own)

    def body(i, carry):
        total = row_product(table, index_ref, i, own_ref, other_ref, half, edge)
        out[i] = (3.0 * table[i].astype(jnp.float32) - 2.0 * total).astype(out.dtype)
        return carry

    lax.fori_loop(0, own, body, 0, unroll=2)


def cube(index, own, other, table, pieces, half):
    size, edge, wide = own.shape
    return pl.pallas_call(
        functools.partial(cube_kernel, half),
        out_shape=[like(own), like(table)],
        in_specs=[SMEM] + [VMEM] * (3 + len(pieces)),
        out_specs=[VMEM] * 2,
        input_output_aliases={3: 1},
        compiler_params=PARAMS,
        cost_estimate=cost(size * 4 * edge * wide * wide, 8 * own.size * 2),
        name="cube_rows",
    )(index, own, other, table, *pieces)[0]


def local(density, columns, kept):
    half = columns.shape[1]
    numbers = everyones(columns, kept)
    other = from_sibling(density)
    rows, *pieces = gather(density, numbers, half)
    got = [from_ahead(piece, step) for step, piece in zip(OFFSETS, pieces)]
    square_index, cube_index, table = tables(numbers, density, other, half)
    got, square_index, cube_index, table = lax.optimization_barrier(
        (got, square_index, cube_index, table)
    )
    got += [from_sibling(piece) for piece in got]
    squares, wanted = square(square_index, rows, density, other, table, got, half)

    got = [from_ahead(piece, step) for step, piece in zip(OFFSETS, wanted)]
    table = stacked(squares, from_sibling(squares))
    got, table = lax.optimization_barrier((got, table))
    got += [from_sibling(piece) for piece in got]
    return cube(cube_index, density, other, table, got, half)


def solution(mesh):
    in_specs = (
        P(("groups", "rows"), None, "layers"),
        P(("groups", "rows"), "layers"),
        P(("groups", "rows"), "layers"),
    )
    out_specs = P(("groups", "rows"), None, "layers")
    return jax.shard_map(local, mesh=mesh, in_specs=in_specs, out_specs=out_specs, check_vma=False)
```

```python
import functools

import jax
import jax.numpy as jnp
from jax import lax
from jax.experimental import pallas as pl
from jax.experimental.pallas import tpu as pltpu
from jax.sharding import PartitionSpec as P

CAP = 2
OFFSETS = (1, -2, -1, 2)
FAR = len(OFFSETS) * CAP
BEHIND = tuple(OFFSETS.index(-step) for step in OFFSETS)
SUBLANES, LANES = 8, 128
VMEM_LIMIT = 40 * 1024 * 1024
PARAMS = pltpu.CompilerParams(vmem_limit_bytes=VMEM_LIMIT)
VMEM = pl.BlockSpec(memory_space=pltpu.VMEM)
SMEM = pl.BlockSpec(memory_space=pltpu.SMEM)


def cost(flops, size):
    return pl.CostEstimate(flops=flops, bytes_accessed=size, transcendentals=0)


def like(value):
    return jax.ShapeDtypeStruct(value.shape, value.dtype)


def from_ahead(value, steps):
    count = lax.axis_size("rows")
    pairs = [(source, (source - steps) % count) for source in range(count)]
    return lax.ppermute(value, "rows", pairs)


def from_sibling(value):
    return lax.ppermute(value, "layers", [(0, 1), (1, 0)])


def stage_kernel(density_ref, staged_ref, sem):
    copy = pltpu.make_async_copy(density_ref, staged_ref, sem)
    copy.start()
    copy.wait()


def stage(density):
    return pl.pallas_call(
        stage_kernel,
        out_shape=like(density),
        in_specs=[pl.BlockSpec(memory_space=pl.ANY)],
        out_specs=VMEM,
        scratch_shapes=[pltpu.SemaphoreType.DMA],
        compiler_params=PARAMS,
        cost_estimate=cost(0, 4 * density.size),
        name="stage_density",
    )(density)


def spread(columns, kept):
    table = jnp.concatenate([columns, kept], axis=1).T
    return jnp.pad(table, ((0, SUBLANES - table.shape[0]), (0, LANES - table.shape[1])))


def named_rows(slots_of_both, owner, own):
    low, high = [], []
    for slots in slots_of_both:
        local = slots - owner * own
        lane = lax.broadcasted_iota(jnp.int32, local.shape, 1)
        inside = (local >= 0) & (local < own) & (lane < own)
        low.append(jnp.where(inside, local, own - 1))
        high.append(jnp.where(inside, local, 0))
    return jnp.minimum(*low), jnp.maximum(*high)


def gather_kernel(half, density_ref, numbers_ref, out):
    both = [numbers_ref[k : k + half] for k in (0, SUBLANES)]
    low, high = named_rows(both, lax.axis_index("rows"), density_ref.shape[0])
    for k, row in enumerate((jnp.min(low), jnp.max(high))):
        out[k] = density_ref[row]


def gather(density, numbers, half):
    own, edge, wide = density.shape
    return pl.pallas_call(
        functools.partial(gather_kernel, half),
        out_shape=jax.ShapeDtypeStruct((CAP, edge, wide), density.dtype),
        in_specs=[VMEM] * 2,
        out_specs=VMEM,
        compiler_params=PARAMS,
        cost_estimate=cost(0, 4 * CAP * edge * wide),
        name="gather_rows",
    )(density, numbers)


def stack(table, own_ref, other_ref, sems):
    own = own_ref.shape[0]
    copies = [
        pltpu.make_async_copy(own_ref, table.at[pl.ds(0, own)], sems.at[0]),
        pltpu.make_async_copy(other_ref, table.at[pl.ds(own, own)], sems.at[1]),
    ]
    for copy in copies:
        copy.start()
    table[table.shape[0] - 1] = jnp.zeros(table.shape[1:], table.dtype)
    return copies


def tables_kernel(half, peers, mine_ref, own_ref, other_ref, *refs):
    near, refs = refs[: len(OFFSETS)], refs[len(OFFSETS) :]
    square_ref, others_ref, cube_ref, table_ref, sems = refs
    own, edge, wide = own_ref.shape
    copies = stack(table_ref, own_ref, other_ref, sems)
    me = lax.axis_index("rows")
    shape = (SUBLANES, LANES)
    lane = lax.broadcasted_iota(jnp.int32, shape, 1)
    pad = jnp.zeros((SUBLANES - 2 * half, LANES), jnp.int32)

    def slots_of(ref):
        return [
            jnp.concatenate(
                [ref[k : k + half], ref[SUBLANES + k : SUBLANES + k + half], pad], axis=0
            )
            for k in (0, half)
        ]

    def bounds(slots_of_both, owner):
        low, high = named_rows(slots_of_both, owner, own)
        low = jnp.min(jnp.min(low, axis=0, keepdims=True), axis=1, keepdims=True)
        high = jnp.max(jnp.max(high, axis=0, keepdims=True), axis=1, keepdims=True)
        return low, high

    columns, kept = slots_of(mine_ref)
    named = (columns[0:half], columns[half : 2 * half])
    column_table, kept_table = columns, kept
    slots = columns - me * own
    for position, step in enumerate(OFFSETS):
        owner = lax.rem(me + step + peers, peers)
        low, high = bounds(named, owner)
        local = columns - owner * own
        first = own + position * CAP
        slots = jnp.where(
            (local >= 0) & (local < own), first + (local != low).astype(jnp.int32), slots
        )
        far_columns, far_kept = slots_of(near[position])
        source = jnp.where(lane == first, low, high)
        here = (lane == first) | (lane == first + 1)
        column_table = jnp.where(
            here, jnp.take_along_axis(far_columns, source, axis=1), column_table
        )
        kept_table = jnp.where(here, jnp.take_along_axis(far_kept, source, axis=1), kept_table)
    asked = jnp.zeros((1, LANES), jnp.int32)
    for position, behind in enumerate(BEHIND):
        numbers = near[behind]
        pair = bounds([numbers[k : k + half] for k in (0, SUBLANES)], me)
        for k in range(CAP):
            asked = jnp.where(lane[0:1] == position * CAP + k, pair[k], asked)
    slots = jnp.where(lane < own, jnp.clip(slots, 0, LANES - 1), 0)
    stride = table_stride(half, edge)
    base = jnp.where(slots < own, slots, slots + own)
    shift = jnp.where(slots < own, own, FAR)
    empty = (table_ref.shape[0] - 1) * stride
    for table, outs in (
        (column_table, ((square_ref, 0), (others_ref, half))),
        (kept_table, ((cube_ref, 0),)),
    ):
        met = [
            jnp.take_along_axis(jnp.broadcast_to(table[b : b + 1], shape), slots, axis=1)
            for b in range(2 * half)
        ]
        for out, first in outs:
            for s in range(half):
                index = jnp.full(shape, empty, jnp.int32)
                for b in range(2 * half):
                    entry = base + shift if b >= half else base
                    place = entry * stride + (b % half) * edge
                    index = jnp.where(met[b] == kept[first + s : first + s + 1], place, index)
                out[s * SUBLANES : (s + 1) * SUBLANES] = index
    square_ref[SUBLANES - 1 : SUBLANES] = asked
    for copy in copies:
        copy.wait()


def table_stride(half, edge):
    return edge << (half - 1).bit_length()


def table_like(own):
    return jax.ShapeDtypeStruct((2 * own.shape[0] + 2 * FAR + 1,) + own.shape[1:], own.dtype)


def tables(mine, near, own, other, half):
    shape = jax.ShapeDtypeStruct((half * SUBLANES, LANES), jnp.int32)
    return pl.pallas_call(
        functools.partial(tables_kernel, half, lax.axis_size("rows")),
        out_shape=[shape, shape, shape, table_like(own)],
        in_specs=[VMEM] * (3 + len(near)),
        out_specs=[VMEM] * 4,
        scratch_shapes=[pltpu.SemaphoreType.DMA((2,))],
        compiler_params=PARAMS,
        cost_estimate=cost(0, 4 * own.size * 2),
        name="block_tables",
    )(mine, own, other, *near)


def others_kernel(half, index_ref, own_ref, other_ref, table_ref, squares_ref, out, sem):
    own, edge, wide = own_ref.shape
    copy = pltpu.make_async_copy(squares_ref, out.at[pl.ds(0, own)], sem)
    copy.start()
    out[out.shape[0] - 1] = jnp.zeros(out.shape[1:], out.dtype)

    def body(i, carry):
        total = row_product(table_ref, index_ref, i, own_ref, other_ref, half, edge)
        out[own + i] = total.astype(out.dtype)
        return carry

    lax.fori_loop(0, own, body, 0, unroll=True)
    copy.wait()


def with_others(index, own, other, table, squares, half):
    size, edge, wide = own.shape
    return pl.pallas_call(
        functools.partial(others_kernel, half),
        out_shape=like(table),
        in_specs=[SMEM] + [VMEM] * 4,
        out_specs=VMEM,
        scratch_shapes=[pltpu.SemaphoreType.DMA],
        compiler_params=PARAMS,
        cost_estimate=cost(size * 4 * edge * wide * wide, 8 * own.size * 2),
        name="square_others",
    )(index, own, other, table, squares)


def add_far(table, pieces, own):
    for position, piece in enumerate(pieces):
        for k in range(CAP):
            table[2 * own + position * CAP + k] = piece[k]


def row_product(table, index_ref, row, own_ref, other_ref, half, edge):
    stride = table_stride(half, edge)

    def left(k):
        ref = own_ref if k < half else other_ref
        return ref[row, :, (k % half) * edge : (k % half + 1) * edge]

    def right(k, s):
        place = index_ref[s * SUBLANES + k, row]
        begin = pl.multiple_of(lax.bitwise_and(place, stride - 1), edge)
        return table[lax.div(place, stride), :, pl.ds(begin, edge)]

    total = None
    for a in range(0, 2 * half, 2):
        pair = range(a, min(a + 2, 2 * half))
        lhs = jnp.concatenate([left(k) for k in pair], axis=1)
        rhs = jnp.concatenate(
            [jnp.concatenate([right(k, s) for s in range(half)], axis=1) for k in pair], axis=0
        )
        term = jnp.dot(lhs, rhs, preferred_element_type=jnp.float32)
        total = term if total is None else total + term
    return total


def square_kernel(half, index_ref, own_ref, other_ref, *refs):
    pieces = refs[1 : 1 + 2 * len(OFFSETS)]
    out, *wanted, table = refs[1 + len(pieces) :]
    own, edge, wide = own_ref.shape
    add_far(table, pieces, own)

    def body(i, carry):
        total = row_product(table, index_ref, i, own_ref, other_ref, half, edge)
        out[i] = total.astype(out.dtype)
        return carry

    lax.fori_loop(0, own, body, 0, unroll=True)
    for position, piece in enumerate(wanted):
        for k in range(CAP):
            piece[k] = out[index_ref[SUBLANES - 1, position * CAP + k]]


def square(index, own, other, table, pieces, half):
    size, edge, wide = own.shape
    piece = jax.ShapeDtypeStruct((CAP, edge, wide), own.dtype)
    count = len(OFFSETS)
    out = pl.pallas_call(
        functools.partial(square_kernel, half),
        out_shape=[like(own), *([piece] * count), like(table)],
        in_specs=[SMEM] + [VMEM] * (3 + len(pieces)),
        out_specs=[VMEM] * (2 + count),
        input_output_aliases={3: 1 + count},
        compiler_params=PARAMS,
        cost_estimate=cost(size * 4 * edge * wide * wide, 8 * own.size * 2),
        name="square_rows",
    )(index, own, other, table, *pieces)
    return out[0], out[1 : 1 + count], out[1 + count]


def cube_kernel(half, index_ref, own_ref, other_ref, *refs):
    pieces = refs[1 : 1 + 2 * len(OFFSETS)]
    result, table, out, sems = refs[1 + len(pieces) :]
    own, edge, wide = own_ref.shape
    add_far(table, pieces, own)

    def written(i):
        return pltpu.make_async_copy(out.at[i], result.at[i], sems.at[i])

    def body(i, carry):
        total = row_product(table, index_ref, i, own_ref, other_ref, half, edge)
        out[i] = (3.0 * table[i].astype(jnp.float32) - 2.0 * total).astype(out.dtype)
        written(i).start()
        return carry

    lax.fori_loop(0, own, body, 0, unroll=True)
    for i in range(own):
        written(i).wait()


def cube(index, own, other, table, pieces, half):
    size, edge, wide = own.shape
    return pl.pallas_call(
        functools.partial(cube_kernel, half),
        out_shape=[like(own), like(table)],
        in_specs=[SMEM] + [VMEM] * (3 + len(pieces)),
        out_specs=[pl.BlockSpec(memory_space=pl.ANY), VMEM],
        input_output_aliases={3: 1},
        scratch_shapes=[pltpu.VMEM(own.shape, own.dtype), pltpu.SemaphoreType.DMA((size,))],
        compiler_params=PARAMS,
        cost_estimate=cost(size * 4 * edge * wide * wide, 8 * own.size * 2),
        name="cube_rows",
    )(index, own, other, table, *pieces)[0]


def local(density, columns, kept):
    half = columns.shape[1]
    other = from_sibling(density)
    numbers = spread(columns, kept)
    mine = jnp.concatenate([numbers, from_sibling(numbers)], axis=0)
    mine, own = lax.optimization_barrier((mine, stage(density)))
    near = [from_ahead(mine, step) for step in OFFSETS]
    pieces = [gather(own, near[behind], half) for behind in BEHIND]
    got = [from_ahead(piece, step) for step, piece in zip(OFFSETS, pieces)]
    *indices, table = tables(mine, near, own, other, half)
    got = [lax.optimization_barrier((piece, table))[0] for piece in got]
    got += [from_sibling(piece) for piece in got]
    square_index, others_index, cube_index = indices
    squares, wanted, table = square(square_index, own, other, table, got, half)

    got = [from_ahead(piece, step) for step, piece in zip(OFFSETS, wanted)]
    table = with_others(others_index, own, other, table, squares, half)
    got = [lax.optimization_barrier((piece, table))[0] for piece in got]
    got += [from_sibling(piece) for piece in got]
    return cube(cube_index, own, other, table, got, half)


def solution(mesh):
    in_specs = (
        P(("groups", "rows"), None, "layers"),
        P(("groups", "rows"), "layers"),
        P(("groups", "rows"), "layers"),
    )
    out_specs = P(("groups", "rows"), None, "layers")
    return jax.shard_map(local, mesh=mesh, in_specs=in_specs, out_specs=out_specs, check_vma=False)
```

```python
import functools

import jax
import jax.numpy as jnp
from jax import lax
from jax.experimental import pallas as pl
from jax.experimental.pallas import tpu as pltpu
from jax.sharding import PartitionSpec as P

CAP = 2
EXCHANGES = ((1, 1), (2, 1), (1, 0), (2, 0))
FAR = len(EXCHANGES) * CAP
SUBLANES, LANES = 8, 128
VMEM_LIMIT = 12 * 1024 * 1024
PARAMS = pltpu.CompilerParams(vmem_limit_bytes=VMEM_LIMIT)
VMEM = pl.BlockSpec(memory_space=pltpu.VMEM)
SMEM = pl.BlockSpec(memory_space=pltpu.SMEM)


def cost(flops, size):
    return pl.CostEstimate(flops=flops, bytes_accessed=size, transcendentals=0)


def like(value):
    return jax.ShapeDtypeStruct(value.shape, value.dtype)


def partner(device, exchange, count):
    reach, phase = exchange
    return (device + reach * (1 - 2 * ((device // reach + phase) % 2)) + count) % count


def swapped(value, exchange):
    count = lax.axis_size("rows")
    pairs = [(source, partner(source, exchange, count)) for source in range(count)]
    return lax.ppermute(value, "rows", pairs)


def from_sibling(value):
    return lax.ppermute(value, "layers", [(0, 1), (1, 0)])


def stage_kernel(density_ref, staged_ref, sem):
    copy = pltpu.make_async_copy(density_ref, staged_ref, sem)
    copy.start()
    copy.wait()


def stage(density):
    return pl.pallas_call(
        stage_kernel,
        out_shape=like(density),
        in_specs=[pl.BlockSpec(memory_space=pl.ANY)],
        out_specs=VMEM,
        scratch_shapes=[pltpu.SemaphoreType.DMA],
        compiler_params=PARAMS,
        cost_estimate=cost(0, 4 * density.size),
        name="stage_density",
    )(density)


def spread(columns, kept):
    table = jnp.concatenate([columns, kept], axis=1).T
    return jnp.pad(table, ((0, SUBLANES - table.shape[0]), (0, LANES - table.shape[1])))


def named_rows(slots_of_both, owner, own):
    low, high = [], []
    for slots in slots_of_both:
        local = slots - owner * own
        lane = lax.broadcasted_iota(jnp.int32, local.shape, 1)
        inside = (local >= 0) & (local < own) & (lane < own)
        low.append(jnp.where(inside, local, own - 1))
        high.append(jnp.where(inside, local, 0))
    return jnp.minimum(*low), jnp.maximum(*high)


def gather_kernel(half, density_ref, numbers_ref, out):
    both = [numbers_ref[k : k + half] for k in (0, SUBLANES)]
    low, high = named_rows(both, lax.axis_index("rows"), density_ref.shape[0])
    for k, row in enumerate((jnp.min(low), jnp.max(high))):
        out[k] = density_ref[row]


def gather(density, numbers, half):
    own, edge, wide = density.shape
    return pl.pallas_call(
        functools.partial(gather_kernel, half),
        out_shape=jax.ShapeDtypeStruct((CAP, edge, wide), density.dtype),
        in_specs=[VMEM] * 2,
        out_specs=VMEM,
        compiler_params=PARAMS,
        cost_estimate=cost(0, 4 * CAP * edge * wide),
        name="gather_rows",
    )(density, numbers)


def stack(table, own_ref, other_ref, sems):
    own = own_ref.shape[0]
    copies = [
        pltpu.make_async_copy(own_ref, table.at[pl.ds(0, own)], sems.at[0]),
        pltpu.make_async_copy(other_ref, table.at[pl.ds(own, own)], sems.at[1]),
    ]
    for copy in copies:
        copy.start()
    table[table.shape[0] - 1] = jnp.zeros(table.shape[1:], table.dtype)
    return copies


def tables_kernel(half, peers, mine_ref, own_ref, other_ref, *refs):
    near, refs = refs[: len(EXCHANGES)], refs[len(EXCHANGES) :]
    square_ref, others_ref, cube_ref, table_ref, sems = refs
    own, edge, wide = own_ref.shape
    copies = stack(table_ref, own_ref, other_ref, sems)
    me = lax.axis_index("rows")
    shape = (SUBLANES, LANES)
    lane = lax.broadcasted_iota(jnp.int32, shape, 1)
    pad = jnp.zeros((SUBLANES - 2 * half, LANES), jnp.int32)

    def slots_of(ref):
        return [
            jnp.concatenate(
                [ref[k : k + half], ref[SUBLANES + k : SUBLANES + k + half], pad], axis=0
            )
            for k in (0, half)
        ]

    def bounds(slots_of_both, owner):
        low, high = named_rows(slots_of_both, owner, own)
        low = jnp.min(jnp.min(low, axis=0, keepdims=True), axis=1, keepdims=True)
        high = jnp.max(jnp.max(high, axis=0, keepdims=True), axis=1, keepdims=True)
        return low, high

    columns, kept = slots_of(mine_ref)
    named = (columns[0:half], columns[half : 2 * half])
    column_table, kept_table = columns, kept
    slots = columns - me * own
    for position, exchange in enumerate(EXCHANGES):
        owner = partner(me, exchange, peers)
        low, high = bounds(named, owner)
        local = columns - owner * own
        first = own + position * CAP
        slots = jnp.where(
            (local >= 0) & (local < own), first + (local != low).astype(jnp.int32), slots
        )
        far_columns, far_kept = slots_of(near[position])
        source = jnp.where(lane == first, low, high)
        here = (lane == first) | (lane == first + 1)
        column_table = jnp.where(
            here, jnp.take_along_axis(far_columns, source, axis=1), column_table
        )
        kept_table = jnp.where(here, jnp.take_along_axis(far_kept, source, axis=1), kept_table)
    asked = jnp.zeros((1, LANES), jnp.int32)
    for position, numbers in enumerate(near):
        pair = bounds([numbers[k : k + half] for k in (0, SUBLANES)], me)
        for k in range(CAP):
            asked = jnp.where(lane[0:1] == position * CAP + k, pair[k], asked)
    slots = jnp.where(lane < own, jnp.clip(slots, 0, LANES - 1), 0)
    stride = table_stride(half, edge)
    base = jnp.where(slots < own, slots, slots + own)
    shift = jnp.where(slots < own, own, FAR)
    empty = (table_ref.shape[0] - 1) * stride

    def met_in(table):
        return [
            jnp.take_along_axis(jnp.broadcast_to(table[b : b + 1], shape), slots, axis=1)
            for b in range(2 * half)
        ]

    def choose(met, target, place, otherwise):
        index = jnp.full(shape, otherwise, jnp.int32)
        for b in range(2 * half):
            index = jnp.where(met[b] == kept[target : target + 1], place(b), index)
        return index

    def place(b):
        return (base + shift if b >= half else base) * stride + (b % half) * edge

    met = met_in(column_table)
    for out, first in ((square_ref, 0), (others_ref, half)):
        for s in range(half):
            out[s * SUBLANES : (s + 1) * SUBLANES] = choose(met, first + s, place, empty)

    met = met_in(kept_table)
    for s in range(half):
        cube_ref[s * SUBLANES : (s + 1) * SUBLANES] = choose(met, s, place, empty)
    square_ref[SUBLANES - 1 : SUBLANES] = asked
    for copy in copies:
        copy.wait()


def table_stride(half, edge):
    return edge << (half - 1).bit_length()


def table_like(own):
    return jax.ShapeDtypeStruct((2 * own.shape[0] + 2 * FAR + 1,) + own.shape[1:], own.dtype)


def tables(mine, near, own, other, half):
    shape = jax.ShapeDtypeStruct((half * SUBLANES, LANES), jnp.int32)
    return pl.pallas_call(
        functools.partial(tables_kernel, half, lax.axis_size("rows")),
        out_shape=[shape, shape, shape, table_like(own)],
        in_specs=[VMEM] * (3 + len(near)),
        out_specs=[VMEM] * 4,
        scratch_shapes=[pltpu.SemaphoreType.DMA((2,))],
        compiler_params=PARAMS,
        cost_estimate=cost(0, 4 * own.size * 2),
        name="block_tables",
    )(mine, own, other, *near)


def add_far(table, begin, own_half, other_half):
    count = len(own_half) * CAP
    for first, pieces in ((begin, own_half), (begin + count, other_half)):
        for position, piece in enumerate(pieces):
            for k in range(CAP):
                table[first + position * CAP + k] = piece[k]


def block_at(table, place, stride, edge):
    begin = pl.multiple_of(lax.bitwise_and(place, stride - 1), edge)
    return table[lax.div(place, stride), :, pl.ds(begin, edge)]


def product(left, right, count, half):
    total = None
    for a in range(0, count, 2):
        pair = range(a, min(a + 2, count))
        lhs = jnp.concatenate([left(k) for k in pair], axis=1)
        rhs = jnp.concatenate(
            [jnp.concatenate([right(k, s) for s in range(half)], axis=1) for k in pair], axis=0
        )
        term = jnp.dot(lhs, rhs, preferred_element_type=jnp.float32)
        total = term if total is None else total + term
    return total


def row_product(table, index_ref, row, own_ref, other_ref, half, edge):
    stride = table_stride(half, edge)

    def left(k):
        ref = own_ref if k < half else other_ref
        return ref[row, :, (k % half) * edge : (k % half + 1) * edge]

    def right(k, s):
        return block_at(table, index_ref[s * SUBLANES + k, row], stride, edge)

    return product(left, right, 2 * half, half)


def wanted_kernel(half, index_ref, own_ref, other_ref, *refs):
    pieces = refs[1 : 1 + 2 * len(EXCHANGES)]
    *wanted, table = refs[1 + len(pieces) :]
    own, edge, wide = own_ref.shape
    add_far(table, 2 * own, pieces[: len(EXCHANGES)], pieces[len(EXCHANGES) :])
    for position, piece in enumerate(wanted):
        for k in range(CAP):
            row = index_ref[SUBLANES - 1, position * CAP + k]
            total = row_product(table, index_ref, row, own_ref, other_ref, half, edge)
            piece[k] = total.astype(piece.dtype)


def square_wanted(index, own, other, table, pieces, half):
    size, edge, wide = own.shape
    piece = jax.ShapeDtypeStruct((CAP, edge, wide), own.dtype)
    count = len(EXCHANGES)
    *wanted, table = pl.pallas_call(
        functools.partial(wanted_kernel, half),
        out_shape=[*([piece] * count), like(table)],
        in_specs=[SMEM] + [VMEM] * (3 + len(pieces)),
        out_specs=[VMEM] * (1 + count),
        input_output_aliases={3: count},
        compiler_params=PARAMS,
        cost_estimate=cost(FAR * 4 * edge * wide * wide, 8 * own.size * 2),
        name="square_wanted",
    )(index, own, other, table, *pieces)
    return wanted, table


def square_kernel(half, index_ref, others_ref, own_ref, other_ref, table_ref, out):
    own, edge, wide = own_ref.shape
    out[out.shape[0] - 1] = jnp.zeros(out.shape[1:], out.dtype)

    def body(i, carry):
        for first, index in ((0, index_ref), (own, others_ref)):
            total = row_product(table_ref, index, i, own_ref, other_ref, half, edge)
            out[first + i] = total.astype(out.dtype)
        return carry

    lax.fori_loop(0, own, body, 0, unroll=4)


def square(index, others, own, other, table, half):
    size, edge, wide = own.shape
    return pl.pallas_call(
        functools.partial(square_kernel, half),
        out_shape=like(table),
        in_specs=[SMEM] * 2 + [VMEM] * 3,
        out_specs=VMEM,
        compiler_params=PARAMS,
        cost_estimate=cost(size * 8 * edge * wide * wide, 8 * own.size * 2),
        name="square_rows",
    )(index, others, own, other, table)


def cube_kernel(half, index_ref, own_ref, other_ref, *refs):
    pieces = refs[1 : 1 + 2 * len(EXCHANGES)]
    result, table, out, sems = refs[1 + len(pieces) :]
    own, edge, wide = own_ref.shape
    add_far(table, 2 * own, pieces[: len(EXCHANGES)], pieces[len(EXCHANGES) :])

    def written(i):
        return pltpu.make_async_copy(out.at[i], result.at[i], sems.at[i])

    def body(i, carry):
        total = row_product(table, index_ref, i, own_ref, other_ref, half, edge)
        out[i] = (3.0 * table[i].astype(jnp.float32) - 2.0 * total).astype(out.dtype)
        written(i).start()
        return carry

    lax.fori_loop(0, own, body, 0, unroll=True)
    for i in range(own):
        written(i).wait()


def cube(index, own, other, table, pieces, half):
    size, edge, wide = own.shape
    return pl.pallas_call(
        functools.partial(cube_kernel, half),
        out_shape=[like(own), like(table)],
        in_specs=[SMEM] + [VMEM] * (3 + len(pieces)),
        out_specs=[pl.BlockSpec(memory_space=pl.ANY), VMEM],
        input_output_aliases={3: 1},
        scratch_shapes=[pltpu.VMEM(own.shape, own.dtype), pltpu.SemaphoreType.DMA((size,))],
        compiler_params=PARAMS,
        cost_estimate=cost(size * 4 * edge * wide * wide, 8 * own.size * 2),
        name="cube_rows",
    )(index, own, other, table, *pieces)[0]


def local(density, columns, kept):
    half = columns.shape[1]
    other = from_sibling(density)
    numbers = spread(columns, kept)
    mine = jnp.concatenate([numbers, from_sibling(numbers)], axis=0)
    mine, own = lax.optimization_barrier((mine, stage(density)))
    near = [swapped(mine, exchange) for exchange in EXCHANGES]
    pieces = [gather(own, numbers, half) for numbers in near]
    got = [swapped(piece, exchange) for exchange, piece in zip(EXCHANGES, pieces)]
    *indices, table = tables(mine, near, own, other, half)
    got = [lax.optimization_barrier((piece, table))[0] for piece in got]
    got += [from_sibling(piece) for piece in got]
    square_index, others_index, cube_index = indices
    wanted, table = square_wanted(square_index, own, other, table, got, half)

    got = [swapped(piece, exchange) for exchange, piece in zip(EXCHANGES, wanted)]
    squares = square(square_index, others_index, own, other, table, half)
    got = [lax.optimization_barrier((piece, squares))[0] for piece in got]
    got += [from_sibling(piece) for piece in got]
    return cube(cube_index, own, other, squares, got, half)


def solution(mesh):
    in_specs = (
        P(("groups", "rows"), None, "layers"),
        P(("groups", "rows"), "layers"),
        P(("groups", "rows"), "layers"),
    )
    out_specs = P(("groups", "rows"), None, "layers")
    return jax.shard_map(local, mesh=mesh, in_specs=in_specs, out_specs=out_specs, check_vma=False)
```

```python
import functools

import jax
import jax.numpy as jnp
from jax import lax
from jax.experimental import pallas as pl
from jax.experimental.pallas import tpu as pltpu
from jax.sharding import PartitionSpec as P

CAP = 2
EXCHANGES = ((1, 1), (2, 1), (1, 0), (2, 0))
FAR = len(EXCHANGES) * CAP
SUBLANES, LANES = 8, 128
VMEM_LIMIT = 12 * 1024 * 1024
PARAMS = pltpu.CompilerParams(vmem_limit_bytes=VMEM_LIMIT)
VMEM = pl.BlockSpec(memory_space=pltpu.VMEM)
SMEM = pl.BlockSpec(memory_space=pltpu.SMEM)


def cost(flops, size):
    return pl.CostEstimate(flops=flops, bytes_accessed=size, transcendentals=0)


def like(value):
    return jax.ShapeDtypeStruct(value.shape, value.dtype)


def partner(device, exchange, count):
    reach, phase = exchange
    return (device + reach * (1 - 2 * ((device // reach + phase) % 2)) + count) % count


def swapped(value, exchange):
    count = lax.axis_size("rows")
    pairs = [(source, partner(source, exchange, count)) for source in range(count)]
    return lax.ppermute(value, "rows", pairs)


def from_sibling(value):
    return lax.ppermute(value, "layers", [(0, 1), (1, 0)])


def stage_kernel(density_ref, staged_ref, sem):
    copy = pltpu.make_async_copy(density_ref, staged_ref, sem)
    copy.start()
    copy.wait()


def stage(density):
    return pl.pallas_call(
        stage_kernel,
        out_shape=like(density),
        in_specs=[pl.BlockSpec(memory_space=pl.ANY)],
        out_specs=VMEM,
        scratch_shapes=[pltpu.SemaphoreType.DMA],
        compiler_params=PARAMS,
        cost_estimate=cost(0, 4 * density.size),
        name="stage_density",
    )(density)


def spread(columns, kept):
    table = jnp.concatenate([columns, kept], axis=1).T
    return jnp.pad(table, ((0, SUBLANES - table.shape[0]), (0, LANES - table.shape[1])))


def named_rows(slots_of_both, owner, own):
    low, high = [], []
    for slots in slots_of_both:
        local = slots - owner * own
        lane = lax.broadcasted_iota(jnp.int32, local.shape, 1)
        inside = (local >= 0) & (local < own) & (lane < own)
        low.append(jnp.where(inside, local, own - 1))
        high.append(jnp.where(inside, local, 0))
    return jnp.minimum(*low), jnp.maximum(*high)


def gather_kernel(half, density_ref, numbers_ref, out):
    both = [numbers_ref[k : k + half] for k in (0, SUBLANES)]
    low, high = named_rows(both, lax.axis_index("rows"), density_ref.shape[0])
    for k, row in enumerate((jnp.min(low), jnp.max(high))):
        out[k] = density_ref[row]


def gather(density, numbers, half):
    own, edge, wide = density.shape
    return pl.pallas_call(
        functools.partial(gather_kernel, half),
        out_shape=jax.ShapeDtypeStruct((CAP, edge, wide), density.dtype),
        in_specs=[VMEM] * 2,
        out_specs=VMEM,
        compiler_params=PARAMS,
        cost_estimate=cost(0, 4 * CAP * edge * wide),
        name="gather_rows",
    )(density, numbers)


def stack(table, own_ref, other_ref, sems):
    own = own_ref.shape[0]
    copies = [
        pltpu.make_async_copy(own_ref, table.at[pl.ds(0, own)], sems.at[0]),
        pltpu.make_async_copy(other_ref, table.at[pl.ds(own, own)], sems.at[1]),
    ]
    for copy in copies:
        copy.start()
    table[table.shape[0] - 1] = jnp.zeros(table.shape[1:], table.dtype)
    return copies


def tables_kernel(half, peers, mine_ref, own_ref, other_ref, *refs):
    near, refs = refs[: len(EXCHANGES)], refs[len(EXCHANGES) :]
    wanted_ref, square_ref, others_ref, cube_ref, table_ref, sems = refs
    own, edge, wide = own_ref.shape
    copies = stack(table_ref, own_ref, other_ref, sems)
    me = lax.axis_index("rows")
    shape = (SUBLANES, LANES)
    lane = lax.broadcasted_iota(jnp.int32, shape, 1)
    pad = jnp.zeros((SUBLANES - 2 * half, LANES), jnp.int32)

    def slots_of(ref):
        return [
            jnp.concatenate(
                [ref[k : k + half], ref[SUBLANES + k : SUBLANES + k + half], pad], axis=0
            )
            for k in (0, half)
        ]

    def bounds(slots_of_both, owner):
        low, high = named_rows(slots_of_both, owner, own)
        low = jnp.min(jnp.min(low, axis=0, keepdims=True), axis=1, keepdims=True)
        high = jnp.max(jnp.max(high, axis=0, keepdims=True), axis=1, keepdims=True)
        return low, high

    columns, kept = slots_of(mine_ref)
    named = (columns[0:half], columns[half : 2 * half])
    column_table, kept_table = columns, kept
    slots = columns - me * own
    for position, exchange in enumerate(EXCHANGES):
        owner = partner(me, exchange, peers)
        low, high = bounds(named, owner)
        local = columns - owner * own
        first = own + position * CAP
        slots = jnp.where(
            (local >= 0) & (local < own), first + (local != low).astype(jnp.int32), slots
        )
        far_columns, far_kept = slots_of(near[position])
        source = jnp.where(lane == first, low, high)
        here = (lane == first) | (lane == first + 1)
        column_table = jnp.where(
            here, jnp.take_along_axis(far_columns, source, axis=1), column_table
        )
        kept_table = jnp.where(here, jnp.take_along_axis(far_kept, source, axis=1), kept_table)
    asked = jnp.zeros((1, LANES), jnp.int32)
    for position, numbers in enumerate(near):
        pair = bounds([numbers[k : k + half] for k in (0, SUBLANES)], me)
        for k in range(CAP):
            asked = jnp.where(lane[0:1] == position * CAP + k, pair[k], asked)
    slots = jnp.where(lane < own, jnp.clip(slots, 0, LANES - 1), 0)
    stride = table_stride(half, edge)
    base = jnp.where(slots < own, slots, slots + own)
    shift = jnp.where(slots < own, own, FAR)
    empty = (table_ref.shape[0] - 1) * stride

    def met_in(table):
        return [
            jnp.take_along_axis(jnp.broadcast_to(table[b : b + 1], shape), slots, axis=1)
            for b in range(2 * half)
        ]

    def choose(met, target, place, otherwise):
        index = jnp.full(shape, otherwise, jnp.int32)
        for b in range(2 * half):
            index = jnp.where(met[b] == kept[target : target + 1], place(b), index)
        return index

    def place(b):
        return (base + shift if b >= half else base) * stride + (b % half) * edge

    met = met_in(column_table)
    for out, first in ((square_ref, 0), (others_ref, half)):
        for s in range(half):
            out[s * SUBLANES : (s + 1) * SUBLANES] = choose(met, first + s, place, empty)

    met = met_in(kept_table)
    for s in range(half):
        cube_ref[s * SUBLANES : (s + 1) * SUBLANES] = choose(met, s, place, empty)
    asked_all = jnp.broadcast_to(asked, shape)
    for s in range(half):
        rows = slice(s * SUBLANES, (s + 1) * SUBLANES)
        wanted_ref[rows] = jnp.take_along_axis(square_ref[rows], asked_all, axis=1)
    wanted_ref[SUBLANES - 1 : SUBLANES] = asked
    for copy in copies:
        copy.wait()


def table_stride(half, edge):
    return edge << (half - 1).bit_length()


def table_like(own):
    return jax.ShapeDtypeStruct((2 * own.shape[0] + 2 * FAR + 1,) + own.shape[1:], own.dtype)


def tables(mine, near, own, other, half):
    shape = jax.ShapeDtypeStruct((half * SUBLANES, LANES), jnp.int32)
    return pl.pallas_call(
        functools.partial(tables_kernel, half, lax.axis_size("rows")),
        out_shape=[shape, shape, shape, shape, table_like(own)],
        in_specs=[VMEM] * (3 + len(near)),
        out_specs=[VMEM] * 5,
        scratch_shapes=[pltpu.SemaphoreType.DMA((2,))],
        compiler_params=PARAMS,
        cost_estimate=cost(0, 4 * own.size * 2),
        name="block_tables",
    )(mine, own, other, *near)


def add_far(table, begin, own_half, other_half):
    count = len(own_half) * CAP
    for first, pieces in ((begin, own_half), (begin + count, other_half)):
        for position, piece in enumerate(pieces):
            for k in range(CAP):
                table[first + position * CAP + k] = piece[k]


def block_at(table, place, stride, edge):
    begin = pl.multiple_of(lax.bitwise_and(place, stride - 1), edge)
    return table[lax.div(place, stride), :, pl.ds(begin, edge)]


def product(left, right, count, half):
    total = None
    for a in range(0, count, 2):
        pair = range(a, min(a + 2, count))
        lhs = jnp.concatenate([left(k) for k in pair], axis=1)
        rhs = jnp.concatenate(
            [jnp.concatenate([right(k, s) for s in range(half)], axis=1) for k in pair], axis=0
        )
        term = jnp.dot(lhs, rhs, preferred_element_type=jnp.float32)
        total = term if total is None else total + term
    return total


def row_product(table, index_ref, entry, own_ref, other_ref, half, edge, row=None):
    stride = table_stride(half, edge)
    row = entry if row is None else row

    def left(k):
        ref = own_ref if k < half else other_ref
        return ref[row, :, (k % half) * edge : (k % half + 1) * edge]

    def right(k, s):
        return block_at(table, index_ref[s * SUBLANES + k, entry], stride, edge)

    return product(left, right, 2 * half, half)


def wanted_kernel(half, first, far, index_ref, own_ref, other_ref, table_in, *refs):
    pieces, (*wanted, table) = refs[:far], refs[far:] if far else (*refs, table_in)
    own, edge, wide = own_ref.shape
    if far:
        add_far(table, 2 * own, pieces[: far // 2], pieces[far // 2 :])
    for position, piece in enumerate(wanted):
        for k in range(CAP):
            n = (first + position) * CAP + k
            row = index_ref[SUBLANES - 1, n]
            total = row_product(table, index_ref, n, own_ref, other_ref, half, edge, row)
            piece[k] = total.astype(piece.dtype)


def square_wanted(index, own, other, table, pieces, half, first, count):
    size, edge, wide = own.shape
    piece = jax.ShapeDtypeStruct((CAP, edge, wide), own.dtype)
    changed = [like(table)] if pieces else []
    out = pl.pallas_call(
        functools.partial(wanted_kernel, half, first, len(pieces)),
        out_shape=[piece] * count + changed,
        in_specs=[VMEM] * (4 + len(pieces)),
        out_specs=[VMEM] * (count + len(changed)),
        input_output_aliases={3: count} if pieces else {},
        compiler_params=PARAMS,
        cost_estimate=cost(count * CAP * 4 * edge * wide * wide, 8 * own.size * 2),
        name="square_wanted",
    )(index, own, other, table, *pieces)
    return out[:count], out[count] if pieces else table


def square_kernel(half, index_ref, others_ref, own_ref, other_ref, table_ref, out):
    own, edge, wide = own_ref.shape
    out[out.shape[0] - 1] = jnp.zeros(out.shape[1:], out.dtype)

    def body(i, carry):
        for first, index in ((0, index_ref), (own, others_ref)):
            total = row_product(table_ref, index, i, own_ref, other_ref, half, edge)
            out[first + i] = total.astype(out.dtype)
        return carry

    lax.fori_loop(0, own, body, 0, unroll=4)


def square(index, others, own, other, table, half):
    size, edge, wide = own.shape
    return pl.pallas_call(
        functools.partial(square_kernel, half),
        out_shape=like(table),
        in_specs=[SMEM] * 2 + [VMEM] * 3,
        out_specs=VMEM,
        compiler_params=PARAMS,
        cost_estimate=cost(size * 8 * edge * wide * wide, 8 * own.size * 2),
        name="square_rows",
    )(index, others, own, other, table)


def cube_kernel(half, index_ref, own_ref, other_ref, *refs):
    pieces = refs[1 : 1 + 2 * len(EXCHANGES)]
    result, table, out, sems = refs[1 + len(pieces) :]
    own, edge, wide = own_ref.shape
    add_far(table, 2 * own, pieces[: len(EXCHANGES)], pieces[len(EXCHANGES) :])

    def written(i):
        return pltpu.make_async_copy(out.at[i], result.at[i], sems.at[i])

    for i in range(own):
        total = row_product(table, index_ref, i, own_ref, other_ref, half, edge)
        out[i] = (3.0 * table[i].astype(jnp.float32) - 2.0 * total).astype(out.dtype)
        written(i).start()
    for i in range(own):
        written(i).wait()


def cube(index, own, other, table, pieces, half):
    size, edge, wide = own.shape
    return pl.pallas_call(
        functools.partial(cube_kernel, half),
        out_shape=[like(own), like(table)],
        in_specs=[VMEM] * (4 + len(pieces)),
        out_specs=[pl.BlockSpec(memory_space=pl.ANY), VMEM],
        input_output_aliases={3: 1},
        scratch_shapes=[
            pltpu.VMEM(own.shape, own.dtype),
            pltpu.SemaphoreType.DMA((size,)),
        ],
        compiler_params=PARAMS,
        cost_estimate=cost(size * 4 * edge * wide * wide, 8 * own.size * 2),
        name="cube_rows",
    )(index, own, other, table, *pieces)[0]


def local(density, columns, kept):
    half = columns.shape[1]
    numbers = spread(columns, kept)
    mine = jnp.concatenate([numbers, from_sibling(numbers)], axis=0)
    mine, own = lax.optimization_barrier((mine, stage(density)))
    other = from_sibling(own)
    near = [swapped(mine, exchange) for exchange in EXCHANGES]
    pieces = [gather(own, numbers, half) for numbers in near]
    got = [swapped(piece, exchange) for exchange, piece in zip(EXCHANGES, pieces)]
    *indices, table = tables(mine, near, own, other, half)
    got = [lax.optimization_barrier((piece, table))[0] for piece in got]
    got += [from_sibling(piece) for piece in got]
    wanted_index, square_index, others_index, cube_index = indices
    wanted, part = [], len(EXCHANGES) // 2
    for first in range(0, len(EXCHANGES), part):
        more, table = square_wanted(
            wanted_index, own, other, table, [] if first else got, half, first, part
        )
        wanted += more

    got = [swapped(piece, exchange) for exchange, piece in zip(EXCHANGES, wanted)]
    squares = square(square_index, others_index, own, other, table, half)
    got = [lax.optimization_barrier((piece, squares))[0] for piece in got]
    got += [from_sibling(piece) for piece in got]
    return cube(cube_index, own, other, squares, got, half)


def solution(mesh):
    in_specs = (
        P(("groups", "rows"), None, "layers"),
        P(("groups", "rows"), "layers"),
        P(("groups", "rows"), "layers"),
    )
    out_specs = P(("groups", "rows"), None, "layers")
    return jax.shard_map(local, mesh=mesh, in_specs=in_specs, out_specs=out_specs, check_vma=False)
```

```python
import functools

import jax
import jax.numpy as jnp
from jax import lax
from jax.experimental import pallas as pl
from jax.experimental.pallas import tpu as pltpu
from jax.sharding import PartitionSpec as P

CAP = 2
EXCHANGES = ((1, 1), (2, 1), (1, 0), (2, 0))
FAR = len(EXCHANGES) * CAP
SUBLANES, LANES = 8, 128
VMEM_LIMIT = 12 * 1024 * 1024
PARAMS = pltpu.CompilerParams(vmem_limit_bytes=VMEM_LIMIT)
VMEM = pl.BlockSpec(memory_space=pltpu.VMEM)
SMEM = pl.BlockSpec(memory_space=pltpu.SMEM)


def cost(flops, size):
    return pl.CostEstimate(flops=flops, bytes_accessed=size, transcendentals=0)


def like(value):
    return jax.ShapeDtypeStruct(value.shape, value.dtype)


def partner(device, exchange, count):
    reach, phase = exchange
    return (device + reach * (1 - 2 * ((device // reach + phase) % 2)) + count) % count


def swapped(value, exchange):
    count = lax.axis_size("rows")
    pairs = [(source, partner(source, exchange, count)) for source in range(count)]
    return lax.ppermute(value, "rows", pairs)


def from_sibling(value):
    return lax.ppermute(value, "layers", [(0, 1), (1, 0)])


def stage_kernel(density_ref, staged_ref, sem):
    copy = pltpu.make_async_copy(density_ref, staged_ref, sem)
    copy.start()
    copy.wait()


def stage(density):
    return pl.pallas_call(
        stage_kernel,
        out_shape=like(density),
        in_specs=[pl.BlockSpec(memory_space=pl.ANY)],
        out_specs=VMEM,
        scratch_shapes=[pltpu.SemaphoreType.DMA],
        compiler_params=PARAMS,
        cost_estimate=cost(0, 4 * density.size),
        name="stage_density",
    )(density)


def spread(columns, kept):
    table = jnp.concatenate([columns, kept], axis=1).T
    return jnp.pad(table, ((0, SUBLANES - table.shape[0]), (0, LANES - table.shape[1])))


def named_rows(slots_of_both, owner, own):
    low, high = [], []
    for slots in slots_of_both:
        local = slots - owner * own
        lane = lax.broadcasted_iota(jnp.int32, local.shape, 1)
        inside = (local >= 0) & (local < own) & (lane < own)
        low.append(jnp.where(inside, local, own - 1))
        high.append(jnp.where(inside, local, 0))
    return jnp.minimum(*low), jnp.maximum(*high)


def gather_kernel(half, density_ref, numbers_ref, out):
    both = [numbers_ref[k : k + half] for k in (0, SUBLANES)]
    low, high = named_rows(both, lax.axis_index("rows"), density_ref.shape[0])
    for k, row in enumerate((jnp.min(low), jnp.max(high))):
        out[k] = density_ref[row]


def gather(density, numbers, half):
    own, edge, wide = density.shape
    return pl.pallas_call(
        functools.partial(gather_kernel, half),
        out_shape=jax.ShapeDtypeStruct((CAP, edge, wide), density.dtype),
        in_specs=[VMEM] * 2,
        out_specs=VMEM,
        compiler_params=PARAMS,
        cost_estimate=cost(0, 4 * CAP * edge * wide),
        name="gather_rows",
    )(density, numbers)


def stack(table, own_ref, other_ref, sems):
    own = own_ref.shape[0]
    copies = [
        pltpu.make_async_copy(own_ref, table.at[pl.ds(0, own)], sems.at[0]),
        pltpu.make_async_copy(other_ref, table.at[pl.ds(own, own)], sems.at[1]),
    ]
    for copy in copies:
        copy.start()
    table[table.shape[0] - 1] = jnp.zeros(table.shape[1:], table.dtype)
    return copies


def tables_kernel(half, peers, mine_ref, own_ref, other_ref, *refs):
    near, refs = refs[: len(EXCHANGES)], refs[len(EXCHANGES) :]
    wanted_ref, square_ref, others_ref, cube_ref, table_ref, sems = refs
    own, edge, wide = own_ref.shape
    copies = stack(table_ref, own_ref, other_ref, sems)
    me = lax.axis_index("rows")
    shape = (SUBLANES, LANES)
    lane = lax.broadcasted_iota(jnp.int32, shape, 1)
    pad = jnp.zeros((SUBLANES - 2 * half, LANES), jnp.int32)

    def slots_of(ref):
        return [
            jnp.concatenate(
                [ref[k : k + half], ref[SUBLANES + k : SUBLANES + k + half], pad], axis=0
            )
            for k in (0, half)
        ]

    def bounds(slots_of_both, owner):
        low, high = named_rows(slots_of_both, owner, own)
        low = jnp.min(jnp.min(low, axis=0, keepdims=True), axis=1, keepdims=True)
        high = jnp.max(jnp.max(high, axis=0, keepdims=True), axis=1, keepdims=True)
        return low, high

    columns, kept = slots_of(mine_ref)
    named = (columns[0:half], columns[half : 2 * half])
    column_table, kept_table = columns, kept
    slots = columns - me * own
    for position, exchange in enumerate(EXCHANGES):
        owner = partner(me, exchange, peers)
        low, high = bounds(named, owner)
        local = columns - owner * own
        first = own + position * CAP
        slots = jnp.where(
            (local >= 0) & (local < own), first + (local != low).astype(jnp.int32), slots
        )
        far_columns, far_kept = slots_of(near[position])
        source = jnp.where(lane == first, low, high)
        here = (lane == first) | (lane == first + 1)
        column_table = jnp.where(
            here, jnp.take_along_axis(far_columns, source, axis=1), column_table
        )
        kept_table = jnp.where(here, jnp.take_along_axis(far_kept, source, axis=1), kept_table)
    asked = jnp.zeros((1, LANES), jnp.int32)
    for position, numbers in enumerate(near):
        pair = bounds([numbers[k : k + half] for k in (0, SUBLANES)], me)
        for k in range(CAP):
            asked = jnp.where(lane[0:1] == position * CAP + k, pair[k], asked)
    slots = jnp.where(lane < own, jnp.clip(slots, 0, LANES - 1), 0)
    stride = table_stride(half, edge)
    base = jnp.where(slots < own, slots, slots + own)
    shift = jnp.where(slots < own, own, FAR)
    empty = (table_ref.shape[0] - 1) * stride

    def met_in(table):
        return [
            jnp.take_along_axis(jnp.broadcast_to(table[b : b + 1], shape), slots, axis=1)
            for b in range(2 * half)
        ]

    def choose(met, target, place, otherwise):
        index = jnp.full(shape, otherwise, jnp.int32)
        for b in range(2 * half):
            index = jnp.where(met[b] == kept[target : target + 1], place(b), index)
        return index

    def place(b):
        return (base + shift if b >= half else base) * stride + (b % half) * edge

    met = met_in(column_table)
    for out, first in ((square_ref, 0), (others_ref, half)):
        for s in range(half):
            out[s * SUBLANES : (s + 1) * SUBLANES] = choose(met, first + s, place, empty)

    met = met_in(kept_table)
    for s in range(half):
        cube_ref[s * SUBLANES : (s + 1) * SUBLANES] = choose(met, s, place, empty)
    asked_all = jnp.broadcast_to(asked, shape)
    for s in range(half):
        rows = slice(s * SUBLANES, (s + 1) * SUBLANES)
        wanted_ref[rows] = jnp.take_along_axis(square_ref[rows], asked_all, axis=1)
    wanted_ref[SUBLANES - 1 : SUBLANES] = asked
    for copy in copies:
        copy.wait()


def table_stride(half, edge):
    return edge << (half - 1).bit_length()


def table_like(own):
    return jax.ShapeDtypeStruct((2 * own.shape[0] + 2 * FAR + 1,) + own.shape[1:], own.dtype)


def tables(mine, near, own, other, half):
    shape = jax.ShapeDtypeStruct((half * SUBLANES, LANES), jnp.int32)
    return pl.pallas_call(
        functools.partial(tables_kernel, half, lax.axis_size("rows")),
        out_shape=[shape, shape, shape, shape, table_like(own)],
        in_specs=[VMEM] * (3 + len(near)),
        out_specs=[VMEM] * 5,
        scratch_shapes=[pltpu.SemaphoreType.DMA((2,))],
        compiler_params=PARAMS,
        cost_estimate=cost(0, 4 * own.size * 2),
        name="block_tables",
    )(mine, own, other, *near)


def add_far(table, begin, own_half, other_half):
    count = len(own_half) * CAP
    for first, pieces in ((begin, own_half), (begin + count, other_half)):
        for position, piece in enumerate(pieces):
            for k in range(CAP):
                table[first + position * CAP + k] = piece[k]


def block_at(table, place, stride, edge):
    begin = pl.multiple_of(lax.bitwise_and(place, stride - 1), edge)
    return table[lax.div(place, stride), :, pl.ds(begin, edge)]


def product(left, right, count, half):
    total = None
    for a in range(0, count, 2):
        pair = range(a, min(a + 2, count))
        lhs = jnp.concatenate([left(k) for k in pair], axis=1)
        rhs = jnp.concatenate(
            [jnp.concatenate([right(k, s) for s in range(half)], axis=1) for k in pair], axis=0
        )
        term = jnp.dot(lhs, rhs, preferred_element_type=jnp.float32)
        total = term if total is None else total + term
    return total


def row_product(table, index_ref, entry, own_ref, other_ref, half, edge, row=None):
    stride = table_stride(half, edge)
    row = entry if row is None else row

    def left(k):
        ref = own_ref if k < half else other_ref
        return ref[row, :, (k % half) * edge : (k % half + 1) * edge]

    def right(k, s):
        return block_at(table, index_ref[s * SUBLANES + k, entry], stride, edge)

    return product(left, right, 2 * half, half)


def wanted_kernel(half, first, far, index_ref, own_ref, other_ref, table_in, *refs):
    pieces, (*wanted, table) = refs[:far], refs[far:] if far else (*refs, table_in)
    own, edge, wide = own_ref.shape
    if far:
        add_far(table, 2 * own, pieces[: far // 2], pieces[far // 2 :])
    for position, piece in enumerate(wanted):
        for k in range(CAP):
            n = (first + position) * CAP + k
            row = index_ref[SUBLANES - 1, n]
            total = row_product(table, index_ref, n, own_ref, other_ref, half, edge, row)
            piece[k] = total.astype(piece.dtype)


def square_wanted(index, own, other, table, pieces, half, first, count):
    size, edge, wide = own.shape
    piece = jax.ShapeDtypeStruct((CAP, edge, wide), own.dtype)
    changed = [like(table)] if pieces else []
    out = pl.pallas_call(
        functools.partial(wanted_kernel, half, first, len(pieces)),
        out_shape=[piece] * count + changed,
        in_specs=[VMEM] * (4 + len(pieces)),
        out_specs=[VMEM] * (count + len(changed)),
        input_output_aliases={3: count} if pieces else {},
        compiler_params=PARAMS,
        cost_estimate=cost(count * CAP * 4 * edge * wide * wide, 8 * own.size * 2),
        name="square_wanted",
    )(index, own, other, table, *pieces)
    return out[:count], out[count] if pieces else table


def square_kernel(half, index_ref, others_ref, own_ref, other_ref, table_ref, out):
    own, edge, wide = own_ref.shape
    out[out.shape[0] - 1] = jnp.zeros(out.shape[1:], out.dtype)

    def body(i, carry):
        for first, index in ((0, index_ref), (own, others_ref)):
            total = row_product(table_ref, index, i, own_ref, other_ref, half, edge)
            out[first + i] = total.astype(out.dtype)
        return carry

    lax.fori_loop(0, own, body, 0, unroll=4)


def square(index, others, own, other, table, half):
    size, edge, wide = own.shape
    return pl.pallas_call(
        functools.partial(square_kernel, half),
        out_shape=like(table),
        in_specs=[SMEM] * 2 + [VMEM] * 3,
        out_specs=VMEM,
        compiler_params=PARAMS,
        cost_estimate=cost(size * 8 * edge * wide * wide, 8 * own.size * 2),
        name="square_rows",
    )(index, others, own, other, table)


def cube_kernel(half, index_ref, own_ref, other_ref, *refs):
    pieces = refs[1 : 1 + 2 * len(EXCHANGES)]
    result, table, out, sems = refs[1 + len(pieces) :]
    own, edge, wide = own_ref.shape
    add_far(table, 2 * own, pieces[: len(EXCHANGES)], pieces[len(EXCHANGES) :])

    def written(i):
        return pltpu.make_async_copy(out.at[i], result.at[i], sems.at[i])

    for i in range(own):
        total = row_product(table, index_ref, i, own_ref, other_ref, half, edge)
        out[i] = (3.0 * table[i].astype(jnp.float32) - 2.0 * total).astype(out.dtype)
        written(i).start()
    for i in range(own):
        written(i).wait()


def cube(index, own, other, table, pieces, half):
    size, edge, wide = own.shape
    return pl.pallas_call(
        functools.partial(cube_kernel, half),
        out_shape=[like(own), like(table)],
        in_specs=[VMEM] * (4 + len(pieces)),
        out_specs=[pl.BlockSpec(memory_space=pl.ANY), VMEM],
        input_output_aliases={3: 1},
        scratch_shapes=[
            pltpu.VMEM(own.shape, own.dtype),
            pltpu.SemaphoreType.DMA((size,)),
        ],
        compiler_params=PARAMS,
        cost_estimate=cost(size * 4 * edge * wide * wide, 8 * own.size * 2),
        name="cube_rows",
    )(index, own, other, table, *pieces)[0]


def local(density, columns, kept):
    half = columns.shape[1]
    numbers = spread(columns, kept)
    mine = jnp.concatenate([numbers, from_sibling(numbers)], axis=0)
    mine, own = lax.optimization_barrier((mine, stage(density)))
    other = from_sibling(own)
    near = [swapped(mine, exchange) for exchange in EXCHANGES]
    pieces = [gather(own, numbers, half) for numbers in near]
    got = [swapped(piece, exchange) for exchange, piece in zip(EXCHANGES, pieces)]
    *indices, table = tables(mine, near, own, other, half)
    got[0] = lax.optimization_barrier((got[0], table))[0]
    got += [from_sibling(piece) for piece in got]
    wanted_index, square_index, others_index, cube_index = indices
    wanted, part = [], len(EXCHANGES) // 2
    for first in range(0, len(EXCHANGES), part):
        more, table = square_wanted(
            wanted_index, own, other, table, [] if first else got, half, first, part
        )
        wanted += more

    got = [swapped(piece, exchange) for exchange, piece in zip(EXCHANGES, wanted)]
    squares = square(square_index, others_index, own, other, table, half)
    got = [lax.optimization_barrier((piece, squares))[0] for piece in got]
    got += [from_sibling(piece) for piece in got]
    return cube(cube_index, own, other, squares, got, half)


def solution(mesh):
    in_specs = (
        P(("groups", "rows"), None, "layers"),
        P(("groups", "rows"), "layers"),
        P(("groups", "rows"), "layers"),
    )
    out_specs = P(("groups", "rows"), None, "layers")
    return jax.shard_map(local, mesh=mesh, in_specs=in_specs, out_specs=out_specs, check_vma=False)
```

```python
import functools

import jax
import jax.numpy as jnp
from jax import lax
from jax.experimental import pallas as pl
from jax.experimental.pallas import tpu as pltpu
from jax.sharding import PartitionSpec as P

CAP = 2
EXCHANGES = ((1, 1), (2, 1), (1, 0), (2, 0))
FAR = len(EXCHANGES) * CAP
SUBLANES, LANES = 8, 128
VMEM_LIMIT = 12 * 1024 * 1024
PARAMS = pltpu.CompilerParams(vmem_limit_bytes=VMEM_LIMIT)
VMEM = pl.BlockSpec(memory_space=pltpu.VMEM)
SMEM = pl.BlockSpec(memory_space=pltpu.SMEM)


def cost(flops, size):
    return pl.CostEstimate(flops=flops, bytes_accessed=size, transcendentals=0)


def like(value):
    return jax.ShapeDtypeStruct(value.shape, value.dtype)


def partner(device, exchange, count):
    reach, phase = exchange
    return (device + reach * (1 - 2 * ((device // reach + phase) % 2)) + count) % count


def swapped(value, exchange):
    count = lax.axis_size("rows")
    pairs = [(source, partner(source, exchange, count)) for source in range(count)]
    return lax.ppermute(value, "rows", pairs)


def from_sibling(value):
    return lax.ppermute(value, "layers", [(0, 1), (1, 0)])


def stage_kernel(density_ref, staged_ref, sem):
    copy = pltpu.make_async_copy(density_ref, staged_ref, sem)
    copy.start()
    copy.wait()


def stage(density):
    return pl.pallas_call(
        stage_kernel,
        out_shape=like(density),
        in_specs=[pl.BlockSpec(memory_space=pl.ANY)],
        out_specs=VMEM,
        scratch_shapes=[pltpu.SemaphoreType.DMA],
        compiler_params=PARAMS,
        cost_estimate=cost(0, 4 * density.size),
        name="stage_density",
    )(density)


def spread(columns, kept):
    table = jnp.concatenate([columns, kept], axis=1).T
    return jnp.pad(table, ((0, SUBLANES - table.shape[0]), (0, LANES - table.shape[1])))


def named_rows(slots_of_both, owner, own):
    low, high = [], []
    for slots in slots_of_both:
        local = slots - owner * own
        lane = lax.broadcasted_iota(jnp.int32, local.shape, 1)
        inside = (local >= 0) & (local < own) & (lane < own)
        low.append(jnp.where(inside, local, own - 1))
        high.append(jnp.where(inside, local, 0))
    return jnp.minimum(*low), jnp.maximum(*high)


def gather_kernel(half, density_ref, numbers_ref, out):
    both = [numbers_ref[k : k + half] for k in (0, SUBLANES)]
    low, high = named_rows(both, lax.axis_index("rows"), density_ref.shape[0])
    for k, row in enumerate((jnp.min(low), jnp.max(high))):
        out[k] = density_ref[row]


def gather(density, numbers, half):
    own, edge, wide = density.shape
    return pl.pallas_call(
        functools.partial(gather_kernel, half),
        out_shape=jax.ShapeDtypeStruct((CAP, edge, wide), density.dtype),
        in_specs=[VMEM] * 2,
        out_specs=VMEM,
        compiler_params=PARAMS,
        cost_estimate=cost(0, 4 * CAP * edge * wide),
        name="gather_rows",
    )(density, numbers)


def stack(table, own_ref, other_ref, sems):
    own = own_ref.shape[0]
    copies = [
        pltpu.make_async_copy(own_ref, table.at[pl.ds(0, own)], sems.at[0]),
        pltpu.make_async_copy(other_ref, table.at[pl.ds(own, own)], sems.at[1]),
    ]
    for copy in copies:
        copy.start()
    table[table.shape[0] - 1] = jnp.zeros(table.shape[1:], table.dtype)
    return copies


def tables_kernel(half, peers, mine_ref, own_ref, other_ref, *refs):
    near, refs = refs[: len(EXCHANGES)], refs[len(EXCHANGES) :]
    wanted_ref, square_ref, others_ref, cube_ref, table_ref, sems = refs
    own, edge, wide = own_ref.shape
    copies = stack(table_ref, own_ref, other_ref, sems)
    me = lax.axis_index("rows")
    shape = (SUBLANES, LANES)
    lane = lax.broadcasted_iota(jnp.int32, shape, 1)
    pad = jnp.zeros((SUBLANES - 2 * half, LANES), jnp.int32)

    def slots_of(ref):
        return [
            jnp.concatenate(
                [ref[k : k + half], ref[SUBLANES + k : SUBLANES + k + half], pad], axis=0
            )
            for k in (0, half)
        ]

    def bounds(slots_of_both, owner):
        low, high = named_rows(slots_of_both, owner, own)
        low = jnp.min(jnp.min(low, axis=0, keepdims=True), axis=1, keepdims=True)
        high = jnp.max(jnp.max(high, axis=0, keepdims=True), axis=1, keepdims=True)
        return low, high

    columns, kept = slots_of(mine_ref)
    named = (columns[0:half], columns[half : 2 * half])
    column_table, kept_table = columns, kept
    slots = columns - me * own
    for position, exchange in enumerate(EXCHANGES):
        owner = partner(me, exchange, peers)
        low, high = bounds(named, owner)
        local = columns - owner * own
        first = own + position * CAP
        slots = jnp.where(
            (local >= 0) & (local < own), first + (local != low).astype(jnp.int32), slots
        )
        far_columns, far_kept = slots_of(near[position])
        source = jnp.where(lane == first, low, high)
        here = (lane == first) | (lane == first + 1)
        column_table = jnp.where(
            here, jnp.take_along_axis(far_columns, source, axis=1), column_table
        )
        kept_table = jnp.where(here, jnp.take_along_axis(far_kept, source, axis=1), kept_table)
    asked = jnp.zeros((1, LANES), jnp.int32)
    for position, numbers in enumerate(near):
        pair = bounds([numbers[k : k + half] for k in (0, SUBLANES)], me)
        for k in range(CAP):
            asked = jnp.where(lane[0:1] == position * CAP + k, pair[k], asked)
    slots = jnp.where(lane < own, jnp.clip(slots, 0, LANES - 1), 0)
    stride = table_stride(half, edge)
    base = jnp.where(slots < own, slots, slots + own)
    shift = jnp.where(slots < own, own, FAR)
    empty = (table_ref.shape[0] - 1) * stride

    def met_in(table):
        return [
            jnp.take_along_axis(jnp.broadcast_to(table[b : b + 1], shape), slots, axis=1)
            for b in range(2 * half)
        ]

    def choose(met, target, place, otherwise):
        index = jnp.full(shape, otherwise, jnp.int32)
        for b in range(2 * half):
            index = jnp.where(met[b] == kept[target : target + 1], place(b), index)
        return index

    def place(b):
        return (base + shift if b >= half else base) * stride + (b % half) * edge

    met = met_in(column_table)
    for out, first in ((square_ref, 0), (others_ref, half)):
        for s in range(half):
            out[s * SUBLANES : (s + 1) * SUBLANES] = choose(met, first + s, place, empty)

    met = met_in(kept_table)
    for s in range(half):
        cube_ref[s * SUBLANES : (s + 1) * SUBLANES] = choose(met, s, place, empty)
    asked_all = jnp.broadcast_to(asked, shape)
    for s in range(half):
        rows = slice(s * SUBLANES, (s + 1) * SUBLANES)
        wanted_ref[rows] = jnp.take_along_axis(square_ref[rows], asked_all, axis=1)
    wanted_ref[SUBLANES - 1 : SUBLANES] = asked
    for copy in copies:
        copy.wait()


def table_stride(half, edge):
    return edge << (half - 1).bit_length()


def table_like(own):
    return jax.ShapeDtypeStruct((2 * own.shape[0] + 2 * FAR + 1,) + own.shape[1:], own.dtype)


def tables(mine, near, own, other, half):
    shape = jax.ShapeDtypeStruct((half * SUBLANES, LANES), jnp.int32)
    return pl.pallas_call(
        functools.partial(tables_kernel, half, lax.axis_size("rows")),
        out_shape=[shape, shape, shape, shape, table_like(own)],
        in_specs=[VMEM] * (3 + len(near)),
        out_specs=[VMEM] * 5,
        scratch_shapes=[pltpu.SemaphoreType.DMA((2,))],
        compiler_params=PARAMS,
        cost_estimate=cost(0, 4 * own.size * 2),
        name="block_tables",
    )(mine, own, other, *near)


def add_far(table, begin, own_half, other_half):
    count = len(own_half) * CAP
    for first, pieces in ((begin, own_half), (begin + count, other_half)):
        for position, piece in enumerate(pieces):
            for k in range(CAP):
                table[first + position * CAP + k] = piece[k]


def block_at(table, place, stride, edge):
    begin = pl.multiple_of(lax.bitwise_and(place, stride - 1), edge)
    return table[lax.div(place, stride), :, pl.ds(begin, edge)]


def product(left, right, count, half):
    total = None
    for a in range(0, count, 2):
        pair = range(a, min(a + 2, count))
        lhs = jnp.concatenate([left(k) for k in pair], axis=1)
        rhs = jnp.concatenate(
            [jnp.concatenate([right(k, s) for s in range(half)], axis=1) for k in pair], axis=0
        )
        term = jnp.dot(lhs, rhs, preferred_element_type=jnp.float32)
        total = term if total is None else total + term
    return total


def row_product(table, index_ref, entry, own_ref, other_ref, half, edge, row=None):
    stride = table_stride(half, edge)
    row = entry if row is None else row

    def left(k):
        ref = own_ref if k < half else other_ref
        return ref[row, :, (k % half) * edge : (k % half + 1) * edge]

    def right(k, s):
        return block_at(table, index_ref[s * SUBLANES + k, entry], stride, edge)

    return product(left, right, 2 * half, half)


def wanted_kernel(half, first, far, index_ref, own_ref, other_ref, table_in, *refs):
    pieces, (*wanted, table) = refs[:far], refs[far:] if far else (*refs, table_in)
    own, edge, wide = own_ref.shape
    if far:
        add_far(table, 2 * own, pieces[: far // 2], pieces[far // 2 :])
    for position, piece in enumerate(wanted):
        for k in range(CAP):
            n = (first + position) * CAP + k
            row = index_ref[SUBLANES - 1, n]
            total = row_product(table, index_ref, n, own_ref, other_ref, half, edge, row)
            piece[k] = total.astype(piece.dtype)


def square_wanted(index, own, other, table, pieces, half, first, count):
    size, edge, wide = own.shape
    piece = jax.ShapeDtypeStruct((CAP, edge, wide), own.dtype)
    changed = [like(table)] if pieces else []
    out = pl.pallas_call(
        functools.partial(wanted_kernel, half, first, len(pieces)),
        out_shape=[piece] * count + changed,
        in_specs=[VMEM] * (4 + len(pieces)),
        out_specs=[VMEM] * (count + len(changed)),
        input_output_aliases={3: count} if pieces else {},
        compiler_params=PARAMS,
        cost_estimate=cost(count * CAP * 4 * edge * wide * wide, 8 * own.size * 2),
        name="square_wanted",
    )(index, own, other, table, *pieces)
    return out[:count], out[count] if pieces else table


def square_kernel(half, index_ref, others_ref, own_ref, other_ref, table_ref, out):
    own, edge, wide = own_ref.shape
    out[out.shape[0] - 1] = jnp.zeros(out.shape[1:], out.dtype)

    def body(i, carry):
        for first, index in ((0, index_ref), (own, others_ref)):
            total = row_product(table_ref, index, i, own_ref, other_ref, half, edge)
            out[first + i] = total.astype(out.dtype)
        return carry

    lax.fori_loop(0, own, body, 0, unroll=4)


def square(index, others, own, other, table, half):
    size, edge, wide = own.shape
    return pl.pallas_call(
        functools.partial(square_kernel, half),
        out_shape=like(table),
        in_specs=[SMEM] * 2 + [VMEM] * 3,
        out_specs=VMEM,
        compiler_params=PARAMS,
        cost_estimate=cost(size * 8 * edge * wide * wide, 8 * own.size * 2),
        name="square_rows",
    )(index, others, own, other, table)


def cube_kernel(half, index_ref, own_ref, other_ref, *refs):
    pieces = refs[1 : 1 + 2 * len(EXCHANGES)]
    result, table, out, sems = refs[1 + len(pieces) :]
    own, edge, wide = own_ref.shape
    add_far(table, 2 * own, pieces[: len(EXCHANGES)], pieces[len(EXCHANGES) :])

    def written(i):
        return pltpu.make_async_copy(out.at[i], result.at[i], sems.at[i])

    for i in range(own):
        total = row_product(table, index_ref, i, own_ref, other_ref, half, edge)
        out[i] = (3.0 * table[i].astype(jnp.float32) - 2.0 * total).astype(out.dtype)
        written(i).start()
    for i in range(own):
        written(i).wait()


def cube(index, own, other, table, pieces, half):
    size, edge, wide = own.shape
    return pl.pallas_call(
        functools.partial(cube_kernel, half),
        out_shape=[like(own), like(table)],
        in_specs=[VMEM] * (4 + len(pieces)),
        out_specs=[pl.BlockSpec(memory_space=pl.ANY), VMEM],
        input_output_aliases={3: 1},
        scratch_shapes=[
            pltpu.VMEM(own.shape, own.dtype),
            pltpu.SemaphoreType.DMA((size,)),
        ],
        compiler_params=PARAMS,
        cost_estimate=cost(size * 4 * edge * wide * wide, 8 * own.size * 2),
        name="cube_rows",
    )(index, own, other, table, *pieces)[0]


def local(density, columns, kept):
    half = columns.shape[1]
    numbers = spread(columns, kept)
    mine = jnp.concatenate([numbers, from_sibling(numbers)], axis=0)
    mine, own = lax.optimization_barrier((mine, stage(density)))
    other = from_sibling(own)
    near = [swapped(mine, exchange) for exchange in EXCHANGES]
    pieces = [gather(own, numbers, half) for numbers in near]
    got = [swapped(piece, exchange) for exchange, piece in zip(EXCHANGES, pieces)]
    *indices, table = tables(mine, near, own, other, half)
    got[0] = lax.optimization_barrier((got[0], table))[0]
    got += [from_sibling(piece) for piece in got]
    wanted_index, square_index, others_index, cube_index = indices
    wanted = []
    for first, part in ((0, 1), (1, len(EXCHANGES) - 1)):
        more, table = square_wanted(
            wanted_index, own, other, table, [] if first else got, half, first, part
        )
        wanted += more

    got = [swapped(piece, exchange) for exchange, piece in zip(EXCHANGES, wanted)]
    squares = square(square_index, others_index, own, other, table, half)
    got = [lax.optimization_barrier((piece, squares))[0] for piece in got]
    got += [from_sibling(piece) for piece in got]
    return cube(cube_index, own, other, squares, got, half)


def solution(mesh):
    in_specs = (
        P(("groups", "rows"), None, "layers"),
        P(("groups", "rows"), "layers"),
        P(("groups", "rows"), "layers"),
    )
    out_specs = P(("groups", "rows"), None, "layers")
    return jax.shard_map(local, mesh=mesh, in_specs=in_specs, out_specs=out_specs, check_vma=False)
```

```python
import functools

import jax
import jax.numpy as jnp
from jax import lax
from jax.experimental import pallas as pl
from jax.experimental.pallas import tpu as pltpu
from jax.sharding import PartitionSpec as P

CAP = 2
EXCHANGES = ((1, 1), (2, 1), (1, 0), (2, 0))
FAR = len(EXCHANGES) * CAP
SUBLANES, LANES = 8, 128
VMEM_LIMIT = 12 * 1024 * 1024
PARAMS = pltpu.CompilerParams(vmem_limit_bytes=VMEM_LIMIT)
VMEM = pl.BlockSpec(memory_space=pltpu.VMEM)
SMEM = pl.BlockSpec(memory_space=pltpu.SMEM)


def cost(flops, size):
    return pl.CostEstimate(flops=flops, bytes_accessed=size, transcendentals=0)


def like(value):
    return jax.ShapeDtypeStruct(value.shape, value.dtype)


def partner(device, exchange, count):
    reach, phase = exchange
    return (device + reach * (1 - 2 * ((device // reach + phase) % 2)) + count) % count


def swapped(value, exchange):
    count = lax.axis_size("rows")
    pairs = [(source, partner(source, exchange, count)) for source in range(count)]
    return lax.ppermute(value, "rows", pairs)


def from_sibling(value):
    return lax.ppermute(value, "layers", [(0, 1), (1, 0)])


def stage_kernel(density_ref, staged_ref, sem):
    copy = pltpu.make_async_copy(density_ref, staged_ref, sem)
    copy.start()
    copy.wait()


def stage(density):
    return pl.pallas_call(
        stage_kernel,
        out_shape=like(density),
        in_specs=[pl.BlockSpec(memory_space=pl.ANY)],
        out_specs=VMEM,
        scratch_shapes=[pltpu.SemaphoreType.DMA],
        compiler_params=PARAMS,
        cost_estimate=cost(0, 4 * density.size),
        name="stage_density",
    )(density)


def spread(columns, kept):
    table = jnp.concatenate([columns, kept], axis=1).T
    return jnp.pad(table, ((0, SUBLANES - table.shape[0]), (0, LANES - table.shape[1])))


def named_rows(slots_of_both, owner, own):
    low, high = [], []
    for slots in slots_of_both:
        local = slots - owner * own
        lane = lax.broadcasted_iota(jnp.int32, local.shape, 1)
        inside = (local >= 0) & (local < own) & (lane < own)
        low.append(jnp.where(inside, local, own - 1))
        high.append(jnp.where(inside, local, 0))
    return jnp.minimum(*low), jnp.maximum(*high)


def gather_kernel(half, density_ref, numbers_ref, out):
    both = [numbers_ref[k : k + half] for k in (0, SUBLANES)]
    low, high = named_rows(both, lax.axis_index("rows"), density_ref.shape[0])
    for k, row in enumerate((jnp.min(low), jnp.max(high))):
        out[k] = density_ref[row]


def gather(density, numbers, half):
    own, edge, wide = density.shape
    return pl.pallas_call(
        functools.partial(gather_kernel, half),
        out_shape=jax.ShapeDtypeStruct((CAP, edge, wide), density.dtype),
        in_specs=[VMEM] * 2,
        out_specs=VMEM,
        compiler_params=PARAMS,
        cost_estimate=cost(0, 4 * CAP * edge * wide),
        name="gather_rows",
    )(density, numbers)


def stack(table, own_ref, other_ref, sems):
    own = own_ref.shape[0]
    copies = [
        pltpu.make_async_copy(own_ref, table.at[pl.ds(0, own)], sems.at[0]),
        pltpu.make_async_copy(other_ref, table.at[pl.ds(own, own)], sems.at[1]),
    ]
    for copy in copies:
        copy.start()
    table[table.shape[0] - 1] = jnp.zeros(table.shape[1:], table.dtype)
    return copies


def tables_kernel(half, peers, mine_ref, own_ref, other_ref, *refs):
    near, refs = refs[: len(EXCHANGES)], refs[len(EXCHANGES) :]
    wanted_ref, square_ref, others_ref, cube_ref, table_ref, sems = refs
    own, edge, wide = own_ref.shape
    copies = stack(table_ref, own_ref, other_ref, sems)
    me = lax.axis_index("rows")
    shape = (SUBLANES, LANES)
    lane = lax.broadcasted_iota(jnp.int32, shape, 1)
    pad = jnp.zeros((SUBLANES - 2 * half, LANES), jnp.int32)

    def slots_of(ref):
        return [
            jnp.concatenate(
                [ref[k : k + half], ref[SUBLANES + k : SUBLANES + k + half], pad], axis=0
            )
            for k in (0, half)
        ]

    def bounds(slots_of_both, owner):
        low, high = named_rows(slots_of_both, owner, own)
        low = jnp.min(jnp.min(low, axis=0, keepdims=True), axis=1, keepdims=True)
        high = jnp.max(jnp.max(high, axis=0, keepdims=True), axis=1, keepdims=True)
        return low, high

    columns, kept = slots_of(mine_ref)
    named = (columns[0:half], columns[half : 2 * half])
    column_table, kept_table = columns, kept
    slots = columns - me * own
    for position, exchange in enumerate(EXCHANGES):
        owner = partner(me, exchange, peers)
        low, high = bounds(named, owner)
        local = columns - owner * own
        first = own + position * CAP
        slots = jnp.where(
            (local >= 0) & (local < own), first + (local != low).astype(jnp.int32), slots
        )
        far_columns, far_kept = slots_of(near[position])
        source = jnp.where(lane == first, low, high)
        here = (lane == first) | (lane == first + 1)
        column_table = jnp.where(
            here, jnp.take_along_axis(far_columns, source, axis=1), column_table
        )
        kept_table = jnp.where(here, jnp.take_along_axis(far_kept, source, axis=1), kept_table)
    asked = jnp.zeros((1, LANES), jnp.int32)
    for position, numbers in enumerate(near):
        pair = bounds([numbers[k : k + half] for k in (0, SUBLANES)], me)
        for k in range(CAP):
            asked = jnp.where(lane[0:1] == position * CAP + k, pair[k], asked)
    slots = jnp.where(lane < own, jnp.clip(slots, 0, LANES - 1), 0)
    stride = table_stride(half, edge)
    base = jnp.where(slots < own, slots, slots + own)
    shift = jnp.where(slots < own, own, FAR)
    empty = (table_ref.shape[0] - 1) * stride

    def met_in(table):
        return [
            jnp.take_along_axis(jnp.broadcast_to(table[b : b + 1], shape), slots, axis=1)
            for b in range(2 * half)
        ]

    def choose(met, target, place, otherwise):
        index = jnp.full(shape, otherwise, jnp.int32)
        for b in range(2 * half):
            index = jnp.where(met[b] == kept[target : target + 1], place(b), index)
        return index

    def place(b):
        return (base + shift if b >= half else base) * stride + (b % half) * edge

    met = met_in(column_table)
    for out, first in ((square_ref, 0), (others_ref, half)):
        for s in range(half):
            out[s * SUBLANES : (s + 1) * SUBLANES] = choose(met, first + s, place, empty)

    met = met_in(kept_table)
    for s in range(half):
        cube_ref[s * SUBLANES : (s + 1) * SUBLANES] = choose(met, s, place, empty)
    asked_all = jnp.broadcast_to(asked, shape)
    for s in range(half):
        rows = slice(s * SUBLANES, (s + 1) * SUBLANES)
        wanted_ref[rows] = jnp.take_along_axis(square_ref[rows], asked_all, axis=1)
    wanted_ref[SUBLANES - 1 : SUBLANES] = asked
    for copy in copies:
        copy.wait()


def table_stride(half, edge):
    return edge << (half - 1).bit_length()


def table_like(own):
    return jax.ShapeDtypeStruct((2 * own.shape[0] + 2 * FAR + 1,) + own.shape[1:], own.dtype)


def tables(mine, near, own, other, half):
    shape = jax.ShapeDtypeStruct((half * SUBLANES, LANES), jnp.int32)
    return pl.pallas_call(
        functools.partial(tables_kernel, half, lax.axis_size("rows")),
        out_shape=[shape, shape, shape, shape, table_like(own)],
        in_specs=[VMEM] * (3 + len(near)),
        out_specs=[VMEM] * 5,
        scratch_shapes=[pltpu.SemaphoreType.DMA((2,))],
        compiler_params=PARAMS,
        cost_estimate=cost(0, 4 * own.size * 2),
        name="block_tables",
    )(mine, own, other, *near)


def add_far(table, begin, own_half, other_half):
    count = len(own_half) * CAP
    for first, pieces in ((begin, own_half), (begin + count, other_half)):
        for position, piece in enumerate(pieces):
            for k in range(CAP):
                table[first + position * CAP + k] = piece[k]


def block_at(table, place, stride, edge):
    begin = pl.multiple_of(lax.bitwise_and(place, stride - 1), edge)
    return table[lax.div(place, stride), :, pl.ds(begin, edge)]


def product(left, right, count, half):
    total = None
    for a in range(0, count, 2):
        pair = range(a, min(a + 2, count))
        lhs = jnp.concatenate([left(k) for k in pair], axis=1)
        rhs = jnp.concatenate(
            [jnp.concatenate([right(k, s) for s in range(half)], axis=1) for k in pair], axis=0
        )
        term = jnp.dot(lhs, rhs, preferred_element_type=jnp.float32)
        total = term if total is None else total + term
    return total


def row_product(table, index_ref, entry, own_ref, other_ref, half, edge, row=None):
    stride = table_stride(half, edge)
    row = entry if row is None else row

    def left(k):
        ref = own_ref if k < half else other_ref
        return ref[row, :, (k % half) * edge : (k % half + 1) * edge]

    def right(k, s):
        return block_at(table, index_ref[s * SUBLANES + k, entry], stride, edge)

    return product(left, right, 2 * half, half)


def wanted_kernel(half, first, far, index_ref, own_ref, other_ref, table_in, *refs):
    pieces, (*wanted, table) = refs[:far], refs[far:] if far else (*refs, table_in)
    own, edge, wide = own_ref.shape
    if far:
        add_far(table, 2 * own, pieces[: far // 2], pieces[far // 2 :])
    for position, piece in enumerate(wanted):
        for k in range(CAP):
            n = (first + position) * CAP + k
            row = index_ref[SUBLANES - 1, n]
            total = row_product(table, index_ref, n, own_ref, other_ref, half, edge, row)
            piece[k] = total.astype(piece.dtype)


def square_wanted(index, own, other, table, pieces, half, first, count):
    size, edge, wide = own.shape
    piece = jax.ShapeDtypeStruct((CAP, edge, wide), own.dtype)
    changed = [like(table)] if pieces else []
    out = pl.pallas_call(
        functools.partial(wanted_kernel, half, first, len(pieces)),
        out_shape=[piece] * count + changed,
        in_specs=[VMEM] * (4 + len(pieces)),
        out_specs=[VMEM] * (count + len(changed)),
        input_output_aliases={3: count} if pieces else {},
        compiler_params=PARAMS,
        cost_estimate=cost(count * CAP * 4 * edge * wide * wide, 8 * own.size * 2),
        name="square_wanted",
    )(index, own, other, table, *pieces)
    return out[:count], out[count] if pieces else table


def square_kernel(half, index_ref, others_ref, own_ref, other_ref, table_ref, out):
    own, edge, wide = own_ref.shape
    out[out.shape[0] - 1] = jnp.zeros(out.shape[1:], out.dtype)

    def body(i, carry):
        for first, index in ((0, index_ref), (own, others_ref)):
            total = row_product(table_ref, index, i, own_ref, other_ref, half, edge)
            out[first + i] = total.astype(out.dtype)
        return carry

    lax.fori_loop(0, own, body, 0, unroll=4)


def square(index, others, own, other, table, half):
    size, edge, wide = own.shape
    return pl.pallas_call(
        functools.partial(square_kernel, half),
        out_shape=like(table),
        in_specs=[SMEM] * 2 + [VMEM] * 3,
        out_specs=VMEM,
        compiler_params=PARAMS,
        cost_estimate=cost(size * 8 * edge * wide * wide, 8 * own.size * 2),
        name="square_rows",
    )(index, others, own, other, table)


def cube_kernel(half, index_ref, own_ref, other_ref, *refs):
    pieces = refs[1 : 1 + 2 * len(EXCHANGES)]
    result, table, out, sems = refs[1 + len(pieces) :]
    own, edge, wide = own_ref.shape
    add_far(table, 2 * own, pieces[: len(EXCHANGES)], pieces[len(EXCHANGES) :])

    def written(i):
        return pltpu.make_async_copy(out.at[i], result.at[i], sems.at[i])

    for i in range(own):
        total = row_product(table, index_ref, i, own_ref, other_ref, half, edge)
        out[i] = (3.0 * table[i].astype(jnp.float32) - 2.0 * total).astype(out.dtype)
        written(i).start()
    for i in range(own):
        written(i).wait()


def cube(index, own, other, table, pieces, half):
    size, edge, wide = own.shape
    return pl.pallas_call(
        functools.partial(cube_kernel, half),
        out_shape=[like(own), like(table)],
        in_specs=[VMEM] * (4 + len(pieces)),
        out_specs=[pl.BlockSpec(memory_space=pl.ANY), VMEM],
        input_output_aliases={3: 1},
        scratch_shapes=[
            pltpu.VMEM(own.shape, own.dtype),
            pltpu.SemaphoreType.DMA((size,)),
        ],
        compiler_params=PARAMS,
        cost_estimate=cost(size * 4 * edge * wide * wide, 8 * own.size * 2),
        name="cube_rows",
    )(index, own, other, table, *pieces)[0]


def local(density, columns, kept):
    half = columns.shape[1]
    numbers = spread(columns, kept)
    mine = jnp.concatenate([numbers, from_sibling(numbers)], axis=0)
    mine, own = lax.optimization_barrier((mine, stage(density)))
    other = from_sibling(own)
    near = [swapped(mine, exchange) for exchange in EXCHANGES]
    pieces = [gather(own, numbers, half) for numbers in near]
    got = [swapped(piece, exchange) for exchange, piece in zip(EXCHANGES, pieces)]
    *indices, table = tables(mine, near, own, other, half)
    got[0] = lax.optimization_barrier((got[0], table))[0]
    got += [from_sibling(piece) for piece in got]
    wanted_index, square_index, others_index, cube_index = indices
    wanted = []
    for first, part in ((0, 1), (1, len(EXCHANGES) - 1)):
        more, table = square_wanted(
            wanted_index, own, other, table, [] if first else got, half, first, part
        )
        wanted += more

    got = [swapped(piece, exchange) for exchange, piece in zip(EXCHANGES, wanted)]
    squares = square(square_index, others_index, own, other, table, half)
    got[0] = lax.optimization_barrier((got[0], squares))[0]
    got += [from_sibling(piece) for piece in got]
    return cube(cube_index, own, other, squares, got, half)


def solution(mesh):
    in_specs = (
        P(("groups", "rows"), None, "layers"),
        P(("groups", "rows"), "layers"),
        P(("groups", "rows"), "layers"),
    )
    out_specs = P(("groups", "rows"), None, "layers")
    return jax.shard_map(local, mesh=mesh, in_specs=in_specs, out_specs=out_specs, check_vma=False)
```
